32 devices in a mesh: head: 4 (over y, x), qblk: 8 (over z, core).
Axes of the slice: x: 2, y: 2, z: 4, core: 2. Of those that a mesh axis runs over, the one named last changes fastest.
Arguments:
- queries: bfloat16 [16384, 4096], P(('qblk', 'head')), may hold values from -6 to 6
- key_states: bfloat16 [16384, 1024], P(('qblk', 'head')), may hold values from -6 to 6
- value_states: bfloat16 [16384, 1024], P(('qblk', 'head')), may hold values from -6 to 6
- vertical_blocks: int32 [32, 5], replicated, may hold values from 0 to 254, as said below
- slash_offsets: int32 [32, 8], replicated, may hold values from 1 to 64, as said below
Outputs:
- attended: bfloat16 [16384, 4096], P(('qblk', 'head'))
The draws below stay inside these ranges and needn't reach their ends.
Inputs may be any that keep to these rules, and one draw needn't show every extreme that they name: `vertical_blocks`: each head names 5 distinct blocks, among them block 0 and block 254. `slash_offsets`: each head names 8 distinct offsets, among them 1 and 64.
All inputs are finite; a program needn't handle non-finite values.
Results may differ from the reference program's by a relative error of at most 0.0033.
Values may be sent and summed in bfloat16 or wider, within the bound.
A program may use at most 64 MiB of HBM per device.

```python
import jax
import jax.numpy as jnp
from jax import lax

H = 32
KVH = 8
HD = 128
BLK = 64
NV = 5
NS = 8
ROWS_Q = 2048
NB_DEV = 32
SEQ = 16384
NB = 256


def drawn_pair(base_key):
    mixed = jax.random.fold_in(base_key, 7)
    key_list = jax.random.split(mixed, 4)
    query_vals = jnp.clip(1.5 * jax.random.normal(key_list[1], (SEQ, H * HD), jnp.float32), -6.0, 6.0)
    key_vals = jnp.clip(1.5 * jax.random.normal(key_list[3], (SEQ, KVH * HD), jnp.float32), -6.0, 6.0)
    return (query_vals.astype(jnp.float32), key_vals.astype(jnp.float32))


def draw_queries(key, part):
    return drawn_pair(key)[0].astype(jnp.bfloat16)


def draw_key_states(key, part):
    return drawn_pair(key)[1].astype(jnp.bfloat16)


def draw_vertical_blocks(key, part):
    head_keys = jax.random.split(jax.random.fold_in(key, 11), H)

    def pick_middle(head_key):
        return jax.random.permutation(head_key, NB - 3)[:NV - 2] + 1
    middle = jax.vmap(pick_middle)(head_keys).astype(jnp.int32)
    first_col = jnp.zeros((H, 1), jnp.int32)
    last_col = jnp.full((H, 1), NB - 2, jnp.int32)
    return jnp.concatenate([first_col, last_col, middle], axis=1)


def draw_slash_offsets(key, part):
    head_keys = jax.random.split(jax.random.fold_in(key, 13), H)

    def pick_middle(head_key):
        return jax.random.permutation(head_key, 2 * NB_DEV - 2)[:NS - 2] + 2
    middle = jax.vmap(pick_middle)(head_keys).astype(jnp.int32)
    first_col = jnp.ones((H, 1), jnp.int32)
    last_col = jnp.full((H, 1), 2 * NB_DEV, jnp.int32)
    return jnp.concatenate([first_col, last_col, middle], axis=1)


def block_levels(own_key, shape, pieces, least, largest):
    loudness, own = 1.0, jax.random.fold_in(own_key, 6)
    for position, parts in pieces:
        heights = jnp.exp(jax.random.uniform(jax.random.fold_in(own, position), (parts,), jnp.float32, least / len(pieces), largest / len(pieces)))
        loudness = loudness * jnp.repeat(heights, shape[position] // parts).reshape([-1 if axis == position else 1 for axis in range(len(shape))])
    return loudness


def scatter_about(stream_key, dims, deviation, reach, pieces=(), kind=jnp.bfloat16):
    result = jax.random.normal(stream_key, dims, jnp.float32) * deviation
    if len(pieces) > 0:
        result = block_levels(stream_key, dims, pieces, -0.22, 0.18) * result
    return jnp.clip(result, min=-reach, max=reach).astype(kind)


def setup_inputs(seed: int = 0) -> dict:
    splits = jax.random.split(jax.random.key(seed), 6)
    queries = draw_queries(jax.random.fold_in(splits[5], 71), 0)
    key_states = draw_key_states(jax.random.fold_in(splits[5], 71), 0)
    value_states = scatter_about(splits[2], (SEQ, KVH * HD), 1.0, 6.0, ((0, 32),))
    vertical_blocks = draw_vertical_blocks(jax.random.fold_in(splits[5], 71), 0)
    slash_offsets = draw_slash_offsets(jax.random.fold_in(splits[5], 71), 0)
    return dict(queries=queries, key_states=key_states, value_states=value_states, vertical_blocks=vertical_blocks, slash_offsets=slash_offsets)


def attend_group(query_block_list, diagonal_key_block, diagonal_value_block, slash_key_block, slash_value_block, vertical_key_block, vertical_value_block, block_ids, slash_row, vert_row):
    number_format = jnp.float32
    logit_scale = HD ** -0.5
    query_wide_rows = query_block_list.astype(number_format)
    diagonal_scores = jnp.einsum("pwr,pgr->pwg", query_wide_rows, diagonal_key_block.astype(number_format)) * logit_scale
    slash_scores = jnp.einsum("pzf,opwf->pzow", query_wide_rows, slash_key_block.astype(number_format)) * logit_scale
    vertical_scores = jnp.einsum("ihx,zsx->ihzs", query_wide_rows, vertical_key_block.astype(number_format)) * logit_scale
    causal = jnp.arange(BLK)[:, None] >= jnp.arange(BLK)[None, :]
    diagonal_scores = jnp.where(causal[None], diagonal_scores, -jnp.inf)
    slash_ok = (block_ids[:, None] - slash_row[None, :]) >= 0
    slash_scores = jnp.where(slash_ok[:, None, :, None], slash_scores, -jnp.inf)
    block_gap = block_ids[:, None] - vert_row[None, :]
    slash_hit = jnp.any(block_gap[:, :, None] == slash_row[None, None, :], axis=2)
    vert_ok = (block_gap > 0) & jnp.logical_not(slash_hit)
    vertical_scores = jnp.where(vert_ok[:, None, :, None], vertical_scores, -jnp.inf)
    row_max = jnp.maximum(jnp.max(diagonal_scores, axis=2), jnp.maximum(jnp.max(slash_scores, axis=(2, 3)), jnp.max(vertical_scores, axis=(2, 3))))
    diagonal_weights = jnp.exp(diagonal_scores - row_max[:, :, None])
    slash_weights = jnp.exp(slash_scores - row_max[:, :, None, None])
    vertical_weights = jnp.exp(vertical_scores - row_max[:, :, None, None])
    row_total = jnp.sum(diagonal_weights, axis=2) + jnp.sum(slash_weights, axis=(2, 3)) + jnp.sum(vertical_weights, axis=(2, 3))
    diagonal_row_max = lax.optimization_barrier(diagonal_weights.astype(jnp.bfloat16)).astype(number_format)
    slash_row_max = lax.optimization_barrier(slash_weights.astype(jnp.bfloat16)).astype(number_format)
    vertical_row_max = lax.optimization_barrier(vertical_weights.astype(jnp.bfloat16)).astype(number_format)
    weight_total = jnp.einsum("rmt,rtl->rml", diagonal_row_max, diagonal_value_block.astype(number_format))
    weight_total = weight_total + jnp.einsum("mnop,ompj->mnj", slash_row_max, slash_value_block.astype(number_format))
    weight_total = weight_total + jnp.einsum("tiyx,yxf->tif", vertical_row_max, vertical_value_block.astype(number_format))
    return (weight_total / row_total[:, :, None]).astype(jnp.bfloat16)


def reference(queries, key_states, value_states, vertical_blocks, slash_offsets):
    group_rows = min(512, ROWS_Q)
    group_blocks = group_rows // BLK
    front = 2 * ROWS_Q
    ratio_heads = H // KVH

    def one_head(head_id):
        kv_head = head_id // ratio_heads
        q_head = lax.dynamic_slice_in_dim(queries, head_id * HD, HD, 1)
        k_head = lax.dynamic_slice_in_dim(key_states, kv_head * HD, HD, 1)
        v_head = lax.dynamic_slice_in_dim(value_states, kv_head * HD, HD, 1)
        slash_row = slash_offsets[head_id]
        vert_row = vertical_blocks[head_id]
        k_padded = jnp.concatenate([jnp.zeros((front, HD), k_head.dtype), k_head], axis=0)
        v_padded = jnp.concatenate([jnp.zeros((front, HD), v_head.dtype), v_head], axis=0)
        vertical_key_block = k_head.reshape(NB, BLK, HD)[vert_row]
        vertical_value_block = v_head.reshape(NB, BLK, HD)[vert_row]

        def one_group(group_index):
            start_row = (group_index * group_rows).astype(jnp.int32)
            query_block_list = lax.dynamic_slice_in_dim(q_head, start_row, group_rows, 0).reshape(group_blocks, BLK, HD)
            diagonal_key_block = lax.dynamic_slice_in_dim(k_head, start_row, group_rows, 0).reshape(group_blocks, BLK, HD)
            diagonal_value_block = lax.dynamic_slice_in_dim(v_head, start_row, group_rows, 0).reshape(group_blocks, BLK, HD)

            def slash_rows(padded, offset_blocks):
                return lax.dynamic_slice_in_dim(padded, (start_row + front - offset_blocks * BLK).astype(jnp.int32), group_rows, 0)

            slash_key_block = jax.vmap(slash_rows, in_axes=(None, 0))(k_padded, slash_row).reshape(NS, group_blocks, BLK, HD)
            slash_value_block = jax.vmap(slash_rows, in_axes=(None, 0))(v_padded, slash_row).reshape(NS, group_blocks, BLK, HD)
            block_ids = (start_row // BLK + jnp.arange(group_blocks, dtype=jnp.int32)).astype(jnp.int32)
            return attend_group(query_block_list, diagonal_key_block, diagonal_value_block, slash_key_block, slash_value_block, vertical_key_block, vertical_value_block, block_ids, slash_row, vert_row)

        outputs = lax.map(one_group, jnp.arange(SEQ // group_rows, dtype=jnp.int32))
        return outputs.reshape(SEQ, HD)

    heads = lax.map(one_head, jnp.arange(H, dtype=jnp.int32))
    return jnp.transpose(heads, (1, 0, 2)).reshape(SEQ, H * HD)
```

```python
import functools
import math

import jax
import jax.numpy as jnp
from jax import lax
from jax.experimental import pallas as pl
from jax.experimental.pallas import tpu as pltpu
from jax.sharding import PartitionSpec as P

H = 32
KVH = 8
HD = 128
BLK = 64
MASKED = -1e30
VMEM_LIMIT = 48 * 1024 * 1024


def from_behind(value, axis, steps):
    count = lax.axis_size(axis)
    leading, last = (max(0, -steps), min(count, count - steps))
    return lax.ppermute(value, axis, [(source, source + steps) for source in range(leading, last)])


def pick_kernel(group, kv_heads, vert_count, offset_ref, kv_ref, out_ref):
    blocks = kv_ref.shape[0] // BLK
    q_heads = out_ref.shape[0] // (vert_count * BLK)
    for head in range(q_heads):
        k_col = (head // group) * HD
        v_col = (kv_heads + head // group) * HD
        for slot in range(vert_count):
            offset = offset_ref[head * vert_count + slot]
            inside = jnp.logical_and(offset >= 0, offset < blocks)
            start = pl.multiple_of(jnp.clip(offset, 0, blocks - 1) * BLK, BLK)
            row = (head * vert_count + slot) * BLK
            for place, col in ((0, k_col), (HD, v_col)):
                piece = kv_ref[pl.ds(start, BLK), col : col + HD]
                out_ref[row : row + BLK, place : place + HD] = jnp.where(
                    inside, piece, jnp.zeros_like(piece)
                )


def pick_vertical(kv_local, offsets, group, kv_heads):
    q_heads, vert_count = offsets.shape
    return pl.pallas_call(
        functools.partial(pick_kernel, group, kv_heads, vert_count),
        out_shape=jax.ShapeDtypeStruct((q_heads * vert_count * BLK, 2 * HD), kv_local.dtype),
        in_specs=[
            pl.BlockSpec(memory_space=pltpu.SMEM),
            pl.BlockSpec(memory_space=pltpu.VMEM),
        ],
        out_specs=pl.BlockSpec(memory_space=pltpu.VMEM),
        compiler_params=pltpu.CompilerParams(vmem_limit_bytes=VMEM_LIMIT),
        name="pick_vertical",
    )(offsets.reshape(-1), kv_local)


def attend_kernel(slash_ref, q_ref, k_ref, v_ref, vk_ref, vv_ref, bias_ref, out_ref):
    head = pl.program_id(0)
    slash_count = slash_ref.shape[1]
    blocks = q_ref.shape[0] // BLK
    front = k_ref.shape[0] // BLK - blocks
    scale = HD ** (-0.5) * math.log2(math.e)
    rows = lax.broadcasted_iota(jnp.int32, (BLK, 2 * BLK), 0)
    cols = lax.broadcasted_iota(jnp.int32, (BLK, 2 * BLK), 1)
    causal = jnp.where(jnp.logical_and(cols < BLK, cols > rows), MASKED, 0.0).astype(jnp.float32)
    offsets = [0] + [slash_ref[head, slot] for slot in range(slash_count)]
    vert_keys = vk_ref[...]
    vert_values = vv_ref[...]

    def one_block(block, carry):
        row = pl.multiple_of(block * BLK, BLK)
        starts = [pl.multiple_of((front + block - offset) * BLK, BLK) for offset in offsets]
        keys = jnp.concatenate([k_ref[pl.ds(start, BLK), :] for start in starts] + [vert_keys], 0)
        query = q_ref[pl.ds(row, BLK), :]
        scores = lax.dot_general(
            query, keys, (((1,), (1,)), ((), ())), preferred_element_type=jnp.float32
        )
        scores = scores * scale + bias_ref[0, pl.ds(block, 1), :]
        scores = jnp.concatenate([scores[:, : 2 * BLK] + causal, scores[:, 2 * BLK :]], 1)
        row_max = jnp.max(scores, axis=1, keepdims=True)
        weights = jnp.exp2(scores - row_max)
        row_total = jnp.sum(weights, axis=1, keepdims=True)
        values = jnp.concatenate(
            [v_ref[pl.ds(start, BLK), :] for start in starts] + [vert_values], 0
        )
        summed = jnp.dot(
            weights.astype(jnp.bfloat16), values, preferred_element_type=jnp.float32
        )
        out_ref[pl.ds(row, BLK), :] = (summed / row_total).astype(out_ref.dtype)
        return carry

    lax.fori_loop(0, blocks, one_block, 0, unroll=4)


def attend(queries, window, vertical, slash, bias, group, kv_heads):
    rows = queries.shape[0]
    q_heads, blocks, width = bias.shape
    front_rows = window.shape[0]
    vert_rows = vertical.shape[0] // q_heads
    products = 4 * q_heads * rows * width * HD
    return pl.pallas_call(
        attend_kernel,
        out_shape=jax.ShapeDtypeStruct((rows, q_heads * HD), queries.dtype),
        grid_spec=pltpu.PrefetchScalarGridSpec(
            num_scalar_prefetch=1,
            grid=(q_heads,),
            in_specs=[
                pl.BlockSpec((rows, HD), lambda h, s: (0, h)),
                pl.BlockSpec((front_rows, HD), lambda h, s: (0, h // group)),
                pl.BlockSpec((front_rows, HD), lambda h, s: (0, kv_heads + h // group)),
                pl.BlockSpec((vert_rows, HD), lambda h, s: (h, 0)),
                pl.BlockSpec((vert_rows, HD), lambda h, s: (h, 1)),
                pl.BlockSpec((1, blocks, width), lambda h, s: (h, 0, 0)),
            ],
            out_specs=pl.BlockSpec((rows, HD), lambda h, s: (0, h)),
        ),
        compiler_params=pltpu.CompilerParams(
            dimension_semantics=("arbitrary",), vmem_limit_bytes=VMEM_LIMIT
        ),
        cost_estimate=pl.CostEstimate(
            flops=products,
            bytes_accessed=4 * rows * q_heads * HD + 2 * window.size,
            transcendentals=q_heads * rows * width,
        ),
        name="attend",
    )(slash, queries, window, window, vertical, vertical, bias)


def per_device(queries, key_states, value_states, vertical_blocks, slash_offsets):
    head_count = lax.axis_size("head")
    head_index = lax.axis_index("head")
    block_index = lax.axis_index("qblk")
    rows_in = queries.shape[0]
    q_heads = H // head_count
    copies = max(1, head_count // KVH)
    kv_heads = KVH * copies // head_count
    group = q_heads // kv_heads

    def by_head(states):
        split = states.reshape(rows_in, KVH, HD)
        if copies > 1:
            split = jnp.repeat(split, copies, axis=1)
        return split.reshape(rows_in, head_count, kv_heads * HD)

    kv_pair = jnp.concatenate([by_head(key_states), by_head(value_states)], axis=2)
    kv_pair = kv_pair.reshape(rows_in, head_count * 2 * kv_heads * HD)
    kv_local = lax.all_to_all(kv_pair, "head", split_axis=1, concat_axis=0, tiled=True)
    row_count = kv_local.shape[0]
    blocks = row_count // BLK

    vert_mine = lax.dynamic_slice_in_dim(vertical_blocks, head_index * q_heads, q_heads, 0)
    slash_mine = lax.dynamic_slice_in_dim(slash_offsets, head_index * q_heads, q_heads, 0)
    first_block = block_index * blocks
    own_vertical = pick_vertical(kv_local, vert_mine - first_block, group, kv_heads)
    vertical = lax.psum(own_vertical, "qblk")
    two_back = from_behind(kv_local, "qblk", 2)
    one_back = from_behind(kv_local, "qblk", 1)

    block_ids = first_block + jnp.arange(blocks, dtype=jnp.int32)
    slash_ok = block_ids[None, :, None] - slash_mine[:, None, :] >= 0
    block_gap = block_ids[None, :, None] - vert_mine[:, None, :]
    slash_hit = jnp.any(block_gap[:, :, :, None] == slash_mine[:, None, None, :], axis=3)
    vert_ok = (block_gap > 0) & jnp.logical_not(slash_hit)
    allowed = jnp.concatenate([jnp.ones((q_heads, blocks, 1), bool), slash_ok, vert_ok], axis=2)
    bias = jnp.where(allowed, 0.0, MASKED).astype(jnp.float32)
    bias = jnp.broadcast_to(bias[:, :, :, None], bias.shape + (BLK,))
    bias = bias.reshape(q_heads, blocks, -1)

    q_local = lax.all_to_all(queries, "head", split_axis=1, concat_axis=0, tiled=True)
    window = jnp.concatenate([two_back, one_back, kv_local], axis=0)
    attended = attend(q_local, window, vertical, slash_mine, bias, group, kv_heads)
    return lax.all_to_all(attended, "head", split_axis=0, concat_axis=1, tiled=True)


def solution(mesh):
    return jax.shard_map(
        per_device,
        mesh=mesh,
        in_specs=(
            P(("qblk", "head"), None),
            P(("qblk", "head"), None),
            P(("qblk", "head"), None),
            P(),
            P(),
        ),
        out_specs=P(("qblk", "head"), None),
        check_vma=False,
    )
```

```python
import functools
import math

import jax
import jax.numpy as jnp
from jax import lax
from jax.experimental import pallas as pl
from jax.experimental.pallas import tpu as pltpu
from jax.sharding import PartitionSpec as P

H = 32
KVH = 8
HD = 128
BLK = 64
MASKED = -1e30
VMEM_LIMIT = 48 * 1024 * 1024


def from_behind(value, axis, steps):
    count = lax.axis_size(axis)
    leading, last = (max(0, -steps), min(count, count - steps))
    return lax.ppermute(value, axis, [(source, source + steps) for source in range(leading, last)])


def pick_kernel(vert_count, offset_ref, kv_ref, out_ref):
    blocks = kv_ref.shape[0] // BLK
    for slot in range(out_ref.shape[0] // BLK):
        offset = offset_ref[slot]
        inside = jnp.logical_and(offset >= 0, offset < blocks)
        start = pl.multiple_of(jnp.clip(offset, 0, blocks - 1) * BLK, BLK)
        piece = kv_ref[pl.ds(start, BLK), :]
        out_ref[slot * BLK : (slot + 1) * BLK, :] = jnp.where(
            inside, piece, jnp.zeros_like(piece)
        )


def pick_vertical(kv_local, offsets):
    q_heads, vert_count = offsets.shape
    return pl.pallas_call(
        functools.partial(pick_kernel, vert_count),
        out_shape=jax.ShapeDtypeStruct((q_heads * vert_count * BLK, 2 * HD), kv_local.dtype),
        in_specs=[
            pl.BlockSpec(memory_space=pltpu.SMEM),
            pl.BlockSpec(memory_space=pltpu.VMEM),
        ],
        out_specs=pl.BlockSpec(memory_space=pltpu.VMEM),
        compiler_params=pltpu.CompilerParams(vmem_limit_bytes=VMEM_LIMIT),
        name="pick_vertical",
    )(offsets.reshape(-1), kv_local)


def attend_kernel(
    slash_ref,
    odd_ref,
    q_ref,
    two_ref,
    low_ref,
    high_ref,
    own_ref,
    vert_ref,
    bias_ref,
    out_ref,
    window_ref,
):
    head = pl.program_id(0)
    slash_count = slash_ref.shape[1]
    rows = q_ref.shape[0]
    blocks = rows // BLK
    front = 2 * blocks

    @pl.when(head == 0)
    def _():
        window_ref[:rows, :] = two_ref[...]
        window_ref[2 * rows :, :] = own_ref[...]

        @pl.when(odd_ref[0] == 1)
        def _():
            window_ref[rows : 2 * rows, :] = low_ref[...]

        @pl.when(odd_ref[0] == 0)
        def _():
            window_ref[rows : 2 * rows, :] = high_ref[...]

    scale = HD ** (-0.5) * math.log2(math.e)
    row_ids = lax.broadcasted_iota(jnp.int32, (BLK, 2 * BLK), 0)
    col_ids = lax.broadcasted_iota(jnp.int32, (BLK, 2 * BLK), 1)
    hidden = jnp.logical_and(col_ids < BLK, col_ids > row_ids)
    causal = jnp.where(hidden, MASKED, 0.0).astype(jnp.float32)
    offsets = [0] + [slash_ref[head, slot] for slot in range(slash_count)]
    lead = (1 + slash_count) % 2 * BLK
    split = (1 + slash_count) * BLK + lead
    together = 4 if blocks % 4 == 0 else 1

    def one_group(step, carry):
        base = pl.multiple_of(step * together * BLK, BLK)
        shared = lax.dot_general(
            q_ref[pl.ds(base, together * BLK), :],
            vert_ref[lead:, :HD],
            (((1,), (1,)), ((), ())),
            preferred_element_type=jnp.float32,
        )
        sums, totals, shared_weights = [], [], []
        for part in range(together):
            block = step * together + part
            row = pl.multiple_of(block * BLK, BLK)
            starts = [pl.multiple_of((front + block - offset) * BLK, BLK) for offset in offsets]

            def gathered(first):
                pieces = [window_ref[pl.ds(start, BLK), first : first + HD] for start in starts]
                if lead:
                    pieces.append(vert_ref[:lead, first : first + HD])
                return jnp.concatenate(pieces, 0)

            scores = lax.dot_general(
                q_ref[pl.ds(row, BLK), :],
                gathered(0),
                (((1,), (1,)), ((), ())),
                preferred_element_type=jnp.float32,
            )
            scores = scores * scale + bias_ref[0, pl.ds(block, 1), :split]
            scores = jnp.concatenate([scores[:, : 2 * BLK] + causal, scores[:, 2 * BLK :]], 1)
            vert_scores = shared[part * BLK : (part + 1) * BLK] * scale
            vert_scores = vert_scores + bias_ref[0, pl.ds(block, 1), split:]
            row_max = jnp.maximum(
                jnp.max(scores, axis=1, keepdims=True),
                jnp.max(vert_scores, axis=1, keepdims=True),
            )
            weights = jnp.exp2(scores - row_max)
            vert_weights = jnp.exp2(vert_scores - row_max)
            totals.append(
                jnp.sum(weights, axis=1, keepdims=True)
                + jnp.sum(vert_weights, axis=1, keepdims=True)
            )
            shared_weights.append(vert_weights.astype(jnp.bfloat16))
            sums.append(
                jnp.dot(
                    weights.astype(jnp.bfloat16), gathered(HD), preferred_element_type=jnp.float32
                )
            )
        summed = jnp.dot(
            jnp.concatenate(shared_weights, 0),
            vert_ref[lead:, HD:],
            preferred_element_type=jnp.float32,
        )
        summed = summed + jnp.concatenate(sums, 0)
        out_ref[pl.ds(base, together * BLK), :] = (
            summed / jnp.concatenate(totals, 0)
        ).astype(out_ref.dtype)
        return carry

    lax.fori_loop(0, blocks // together, one_group, 0, unroll=2)


def attend(queries, two_back, low, high, own, odd, vertical, slash, bias):
    rows = queries.shape[0]
    q_heads, blocks, width = bias.shape
    vert_rows = vertical.shape[0] // q_heads
    whole = pl.BlockSpec((rows, 2 * HD), lambda h, s, o: (0, 0))
    return pl.pallas_call(
        attend_kernel,
        out_shape=jax.ShapeDtypeStruct((rows, q_heads * HD), queries.dtype),
        grid_spec=pltpu.PrefetchScalarGridSpec(
            num_scalar_prefetch=2,
            grid=(q_heads,),
            in_specs=[
                pl.BlockSpec((rows, HD), lambda h, s, o: (0, h)),
                whole,
                whole,
                whole,
                whole,
                pl.BlockSpec((vert_rows, 2 * HD), lambda h, s, o: (h, 0)),
                pl.BlockSpec((1, blocks, width), lambda h, s, o: (h, 0, 0)),
            ],
            out_specs=pl.BlockSpec((rows, HD), lambda h, s, o: (0, h)),
            scratch_shapes=[pltpu.VMEM((3 * rows, 2 * HD), queries.dtype)],
        ),
        compiler_params=pltpu.CompilerParams(
            dimension_semantics=("arbitrary",), vmem_limit_bytes=VMEM_LIMIT
        ),
        cost_estimate=pl.CostEstimate(
            flops=4 * q_heads * rows * width * HD,
            bytes_accessed=4 * q_heads * blocks * width * HD,
            transcendentals=q_heads * rows * width,
        ),
        name="attend",
    )(slash, odd, queries, two_back, low, high, own, vertical, bias)


def per_device(queries, key_states, value_states, vertical_blocks, slash_offsets):
    head_count = lax.axis_size("head")
    head_index = lax.axis_index("head")
    run_count = lax.axis_size("qblk")
    block_index = lax.axis_index("qblk")
    rows_in = queries.shape[0]
    q_heads = H // head_count
    copies = max(1, head_count // KVH)
    kv_heads = KVH * copies // head_count
    group = q_heads // kv_heads

    wide = group * HD

    def columns(array, first, width):
        return lax.slice_in_dim(array, first, first + width, axis=1)

    def to_heads(pieces):
        flat = jnp.concatenate(pieces, axis=1)
        return lax.all_to_all(flat, "head", split_axis=1, concat_axis=0, tiled=True)

    own = [
        to_heads(
            [
                columns(states, (peer * kv_heads + kv) // copies * HD, HD)
                for peer in range(head_count)
                for states in (key_states, value_states)
            ]
        )
        for kv in range(kv_heads)
    ]
    row_count = own[0].shape[0]
    blocks = row_count // BLK
    vert_mine = lax.dynamic_slice_in_dim(vertical_blocks, head_index * q_heads, q_heads, 0)
    slash_mine = lax.dynamic_slice_in_dim(slash_offsets, head_index * q_heads, q_heads, 0)
    first_block = block_index * blocks
    odd = lax.rem(block_index, 2).astype(jnp.int32).reshape(1)

    block_ids = first_block + jnp.arange(blocks, dtype=jnp.int32)
    slash_ok = block_ids[None, :, None] - slash_mine[:, None, :] >= 0
    block_gap = block_ids[None, :, None] - vert_mine[:, None, :]
    slash_hit = jnp.any(block_gap[:, :, :, None] == slash_mine[:, None, None, :], axis=3)
    vert_ok = (block_gap > 0) & jnp.logical_not(slash_hit)
    allowed = jnp.concatenate([jnp.ones((q_heads, blocks, 1), bool), slash_ok, vert_ok], axis=2)
    bias = jnp.where(allowed, 0.0, MASKED).astype(jnp.float32)
    bias = jnp.broadcast_to(bias[:, :, :, None], bias.shape + (BLK,))
    bias = bias.reshape(q_heads, blocks, -1)

    upward = [(run, run + 1) for run in range(0, run_count - 1, 2)]
    downward = [(run + 1, run) for run in range(0, run_count - 1, 2)]
    returned = []
    for kv in range(kv_heads):
        heads = slice(kv * group, (kv + 1) * group)
        two_back = from_behind(own[kv], "qblk", 2)
        vertical = lax.psum(pick_vertical(own[kv], vert_mine[heads] - first_block), "qblk")
        low = lax.ppermute(own[kv], "qblk", upward)
        q_local = to_heads(
            [columns(queries, (peer * kv_heads + kv) * wide, wide) for peer in range(head_count)]
        )
        high = lax.ppermute(two_back, "qblk", downward)
        attended = attend(
            q_local, two_back, low, high, own[kv], odd, vertical, slash_mine[heads], bias[heads]
        )
        returned.append(
            lax.all_to_all(attended, "head", split_axis=0, concat_axis=1, tiled=True)
        )
    return jnp.concatenate(
        [columns(part, peer * wide, wide) for peer in range(head_count) for part in returned], 1
    )


def solution(mesh):
    return jax.shard_map(
        per_device,
        mesh=mesh,
        in_specs=(
            P(("qblk", "head"), None),
            P(("qblk", "head"), None),
            P(("qblk", "head"), None),
            P(),
            P(),
        ),
        out_specs=P(("qblk", "head"), None),
        check_vma=False,
    )
```

```python
import functools
import math

import jax
import jax.numpy as jnp
from jax import lax
from jax.experimental import pallas as pl
from jax.experimental.pallas import tpu as pltpu
from jax.sharding import PartitionSpec as P

H = 32
KVH = 8
HD = 128
BLK = 64
MASKED = -1e30
VMEM_LIMIT = 48 * 1024 * 1024


def from_behind(value, axis, steps):
    count = lax.axis_size(axis)
    leading, last = (max(0, -steps), min(count, count - steps))
    return lax.ppermute(value, axis, [(source, source + steps) for source in range(leading, last)])


def pick_kernel(group, kv_heads, vert_count, offset_ref, kv_ref, out_ref):
    blocks = kv_ref.shape[0] // BLK
    q_heads = out_ref.shape[0] // (vert_count * BLK)
    for head in range(q_heads):
        k_col = (head // group) * HD
        v_col = (kv_heads + head // group) * HD
        for slot in range(vert_count):
            offset = offset_ref[head * vert_count + slot]
            inside = jnp.logical_and(offset >= 0, offset < blocks)
            start = pl.multiple_of(jnp.clip(offset, 0, blocks - 1) * BLK, BLK)
            row = (head * vert_count + slot) * BLK
            for place, col in ((0, k_col), (HD, v_col)):
                piece = kv_ref[pl.ds(start, BLK), col : col + HD]
                out_ref[row : row + BLK, place : place + HD] = jnp.where(
                    inside, piece, jnp.zeros_like(piece)
                )


def pick_vertical(kv_local, offsets, group, kv_heads):
    q_heads, vert_count = offsets.shape
    return pl.pallas_call(
        functools.partial(pick_kernel, group, kv_heads, vert_count),
        out_shape=jax.ShapeDtypeStruct((q_heads * vert_count * BLK, 2 * HD), kv_local.dtype),
        in_specs=[
            pl.BlockSpec(memory_space=pltpu.SMEM),
            pl.BlockSpec(memory_space=pltpu.VMEM),
        ],
        out_specs=pl.BlockSpec(memory_space=pltpu.VMEM),
        compiler_params=pltpu.CompilerParams(vmem_limit_bytes=VMEM_LIMIT),
        name="pick_vertical",
    )(offsets.reshape(-1), kv_local)


def attend_kernel(
    group,
    kv_heads,
    slash_ref,
    odd_ref,
    q_ref,
    two_ref,
    low_ref,
    high_ref,
    own_ref,
    vert_ref,
    bias_ref,
    out_ref,
    key_ref,
    value_ref,
):
    head = pl.program_id(0)
    slash_count = slash_ref.shape[1]
    rows = q_ref.shape[0]
    blocks = rows // BLK
    front = 2 * blocks

    def load_run(run, ref, kv):
        first = run * rows
        value_ref[first : first + rows, :] = ref[:, (kv_heads + kv) * HD : (kv_heads + kv + 1) * HD]

        def turn(block, carry):
            piece = ref[pl.ds(pl.multiple_of(block * BLK, BLK), BLK), kv * HD : (kv + 1) * HD]
            key_ref[run * blocks + block] = jnp.concatenate([piece, piece], 0).T
            return carry

        lax.fori_loop(0, blocks, turn, 0, unroll=4)

    for kv in range(kv_heads):

        @pl.when(head == kv * group)
        def _():
            load_run(0, two_ref, kv)
            load_run(2, own_ref, kv)

        @pl.when(jnp.logical_and(head == kv * group, odd_ref[0] == 1))
        def _():
            load_run(1, low_ref, kv)

        @pl.when(jnp.logical_and(head == kv * group, odd_ref[0] == 0))
        def _():
            load_run(1, high_ref, kv)

    left = lax.broadcasted_iota(jnp.int32, (HD, 2 * BLK), 1) < BLK
    if (1 + slash_ref.shape[1]) % 2:
        first_vert = vert_ref[:BLK, :HD]
        lead_keys = [jnp.concatenate([first_vert, first_vert], 0).T]
    else:
        lead_keys = []
    scale = HD ** (-0.5) * math.log2(math.e)
    row_ids = lax.broadcasted_iota(jnp.int32, (BLK, 2 * BLK), 0)
    col_ids = lax.broadcasted_iota(jnp.int32, (BLK, 2 * BLK), 1)
    hidden = jnp.logical_and(col_ids < BLK, col_ids > row_ids)
    causal = jnp.where(hidden, MASKED, 0.0).astype(jnp.float32)
    offsets = [0] + [slash_ref[head, slot] for slot in range(slash_count)]
    lead = (1 + slash_count) % 2 * BLK
    split = (1 + slash_count) * BLK + lead
    together = 4 if blocks % 4 == 0 else 1

    def one_group(step, carry):
        base = pl.multiple_of(step * together * BLK, BLK)
        shared = lax.dot_general(
            q_ref[pl.ds(base, together * BLK), :],
            vert_ref[lead:, :HD],
            (((1,), (1,)), ((), ())),
            preferred_element_type=jnp.float32,
        )
        sums, totals, shared_weights = [], [], []
        for part in range(together):
            block = step * together + part
            row = pl.multiple_of(block * BLK, BLK)
            starts = [pl.multiple_of((front + block - offset) * BLK, BLK) for offset in offsets]

            halves = [key_ref[front + block - offset] for offset in offsets] + lead_keys
            keys = [
                jnp.where(left, halves[pair], halves[pair + 1])
                for pair in range(0, len(halves), 2)
            ]
            values = [value_ref[pl.ds(start, BLK), :] for start in starts]
            if lead:
                values.append(vert_ref[:lead, HD:])
            scores = jnp.dot(
                q_ref[pl.ds(row, BLK), :],
                jnp.concatenate(keys, 1),
                preferred_element_type=jnp.float32,
            )
            scores = scores * scale + bias_ref[0, pl.ds(block, 1), :split]
            scores = jnp.concatenate([scores[:, : 2 * BLK] + causal, scores[:, 2 * BLK :]], 1)
            vert_scores = shared[part * BLK : (part + 1) * BLK] * scale
            vert_scores = vert_scores + bias_ref[0, pl.ds(block, 1), split:]
            row_max = jnp.maximum(
                jnp.max(scores, axis=1, keepdims=True),
                jnp.max(vert_scores, axis=1, keepdims=True),
            )
            weights = jnp.exp2(scores - row_max)
            vert_weights = jnp.exp2(vert_scores - row_max)
            totals.append(
                jnp.sum(weights, axis=1, keepdims=True)
                + jnp.sum(vert_weights, axis=1, keepdims=True)
            )
            shared_weights.append(vert_weights.astype(jnp.bfloat16))
            sums.append(
                jnp.dot(
                    weights.astype(jnp.bfloat16),
                    jnp.concatenate(values, 0),
                    preferred_element_type=jnp.float32,
                )
            )
        summed = jnp.dot(
            jnp.concatenate(shared_weights, 0),
            vert_ref[lead:, HD:],
            preferred_element_type=jnp.float32,
        )
        summed = summed + jnp.concatenate(sums, 0)
        out_ref[pl.ds(base, together * BLK), :] = (
            summed / jnp.concatenate(totals, 0)
        ).astype(out_ref.dtype)
        return carry

    lax.fori_loop(0, blocks // together, one_group, 0, unroll=2)


def attend(queries, two_back, low, high, own, odd, vertical, slash, bias, group, kv_heads):
    rows = queries.shape[0]
    q_heads, blocks, width = bias.shape
    vert_rows = vertical.shape[0] // q_heads
    whole = pl.BlockSpec(own.shape, lambda h, s, o: (0, 0))
    return pl.pallas_call(
        functools.partial(attend_kernel, group, kv_heads),
        out_shape=jax.ShapeDtypeStruct((rows, q_heads * HD), queries.dtype),
        grid_spec=pltpu.PrefetchScalarGridSpec(
            num_scalar_prefetch=2,
            grid=(q_heads,),
            in_specs=[
                pl.BlockSpec((rows, HD), lambda h, s, o: (0, h)),
                whole,
                whole,
                whole,
                whole,
                pl.BlockSpec((vert_rows, 2 * HD), lambda h, s, o: (h, 0)),
                pl.BlockSpec((1, blocks, width), lambda h, s, o: (h, 0, 0)),
            ],
            out_specs=pl.BlockSpec((rows, HD), lambda h, s, o: (0, h)),
            scratch_shapes=[
                pltpu.VMEM((3 * blocks, HD, 2 * BLK), queries.dtype),
                pltpu.VMEM((3 * rows, HD), queries.dtype),
            ],
        ),
        compiler_params=pltpu.CompilerParams(
            dimension_semantics=("arbitrary",), vmem_limit_bytes=VMEM_LIMIT
        ),
        cost_estimate=pl.CostEstimate(
            flops=4 * q_heads * rows * width * HD,
            bytes_accessed=4 * q_heads * blocks * width * HD,
            transcendentals=q_heads * rows * width,
        ),
        name="attend",
    )(slash, odd, queries, two_back, low, high, own, vertical, bias)


def per_device(queries, key_states, value_states, vertical_blocks, slash_offsets):
    head_count = lax.axis_size("head")
    head_index = lax.axis_index("head")
    run_count = lax.axis_size("qblk")
    block_index = lax.axis_index("qblk")
    rows_in = queries.shape[0]
    q_heads = H // head_count
    copies = max(1, head_count // KVH)
    kv_heads = KVH * copies // head_count
    group = q_heads // kv_heads

    def by_head(states):
        split = states.reshape(rows_in, KVH, HD)
        if copies > 1:
            split = jnp.repeat(split, copies, axis=1)
        return split.reshape(rows_in, head_count, kv_heads * HD)

    kv_pair = jnp.concatenate([by_head(key_states), by_head(value_states)], axis=2)
    kv_pair = kv_pair.reshape(rows_in, head_count * 2 * kv_heads * HD)
    kv_local = lax.all_to_all(kv_pair, "head", split_axis=1, concat_axis=0, tiled=True)
    row_count = kv_local.shape[0]
    blocks = row_count // BLK
    vert_mine = lax.dynamic_slice_in_dim(vertical_blocks, head_index * q_heads, q_heads, 0)
    slash_mine = lax.dynamic_slice_in_dim(slash_offsets, head_index * q_heads, q_heads, 0)
    first_block = block_index * blocks
    own_vertical = pick_vertical(kv_local, vert_mine - first_block, group, kv_heads)
    own_vertical, queries, vert_mine = lax.optimization_barrier((own_vertical, queries, vert_mine))
    vertical = lax.psum(own_vertical, "qblk")
    odd = lax.rem(block_index, 2).astype(jnp.int32).reshape(1)

    block_ids = first_block + jnp.arange(blocks, dtype=jnp.int32)
    slash_ok = block_ids[None, :, None] - slash_mine[:, None, :] >= 0
    block_gap = block_ids[None, :, None] - vert_mine[:, None, :]
    slash_hit = jnp.any(block_gap[:, :, :, None] == slash_mine[:, None, None, :], axis=3)
    vert_ok = (block_gap > 0) & jnp.logical_not(slash_hit)
    allowed = jnp.concatenate([jnp.ones((q_heads, blocks, 1), bool), slash_ok, vert_ok], axis=2)
    bias = jnp.where(allowed, 0.0, MASKED).astype(jnp.float32)
    bias = jnp.broadcast_to(bias[:, :, :, None], bias.shape + (BLK,))
    bias = bias.reshape(q_heads, blocks, -1)

    upward = [(run, run + 1) for run in range(0, run_count - 1, 2)]
    downward = [(run + 1, run) for run in range(0, run_count - 1, 2)]
    two_back = from_behind(kv_local, "qblk", 2)
    low = lax.ppermute(kv_local, "qblk", upward)
    high = lax.ppermute(two_back, "qblk", downward)
    q_local = lax.all_to_all(queries, "head", split_axis=1, concat_axis=0, tiled=True)
    attended = attend(
        q_local,
        two_back,
        low,
        high,
        kv_local,
        odd,
        vertical,
        slash_mine,
        bias,
        group,
        kv_heads,
    )
    return lax.all_to_all(attended, "head", split_axis=0, concat_axis=1, tiled=True)


def solution(mesh):
    return jax.shard_map(
        per_device,
        mesh=mesh,
        in_specs=(
            P(("qblk", "head"), None),
            P(("qblk", "head"), None),
            P(("qblk", "head"), None),
            P(),
            P(),
        ),
        out_specs=P(("qblk", "head"), None),
        check_vma=False,
    )
```

```python
import functools
import math

import jax
import jax.numpy as jnp
from jax import lax
from jax.experimental import pallas as pl
from jax.experimental.pallas import tpu as pltpu
from jax.sharding import PartitionSpec as P

H = 32
KVH = 8
HD = 128
BLK = 64
MASKED = -1e30
VMEM_LIMIT = 48 * 1024 * 1024


def from_behind(value, axis, steps):
    count = lax.axis_size(axis)
    leading, last = (max(0, -steps), min(count, count - steps))
    return lax.ppermute(value, axis, [(source, source + steps) for source in range(leading, last)])


def pick_kernel(group, kv_heads, vert_count, offset_ref, kv_ref, out_ref):
    blocks = kv_ref.shape[0] // BLK
    q_heads = out_ref.shape[0] // (vert_count * BLK)
    for head in range(q_heads):
        k_col = (head // group) * HD
        v_col = (kv_heads + head // group) * HD
        for slot in range(vert_count):
            offset = offset_ref[head * vert_count + slot]
            inside = jnp.logical_and(offset >= 0, offset < blocks)
            start = pl.multiple_of(jnp.clip(offset, 0, blocks - 1) * BLK, BLK)
            row = (head * vert_count + slot) * BLK
            for place, col in ((0, k_col), (HD, v_col)):
                piece = kv_ref[pl.ds(start, BLK), col : col + HD]
                out_ref[row : row + BLK, place : place + HD] = jnp.where(
                    inside, piece, jnp.zeros_like(piece)
                )


def pick_vertical(kv_local, offsets, group, kv_heads):
    q_heads, vert_count = offsets.shape
    return pl.pallas_call(
        functools.partial(pick_kernel, group, kv_heads, vert_count),
        out_shape=jax.ShapeDtypeStruct((q_heads * vert_count * BLK, 2 * HD), kv_local.dtype),
        in_specs=[
            pl.BlockSpec(memory_space=pltpu.SMEM),
            pl.BlockSpec(memory_space=pltpu.VMEM),
        ],
        out_specs=pl.BlockSpec(memory_space=pltpu.VMEM),
        compiler_params=pltpu.CompilerParams(vmem_limit_bytes=VMEM_LIMIT),
        name="pick_vertical",
    )(offsets.reshape(-1), kv_local)


def chain_kernel(
    pieces,
    own_ref,
    out_ref,
    total_ref,
    inbox_ref,
    carry_ref,
    swap_sems,
    down_sems,
    arrive_sems,
    give_sems,
    take_sems,
):
    run = lax.axis_index("qblk")
    runs = lax.axis_size("qblk")
    core = lax.rem(run, 2)
    partner = run + 1 - 2 * core
    first = run < 2
    last = run >= runs - 2
    half = own_ref.shape[0] // 2
    rows = half // pieces
    mine = pl.multiple_of(core * half, BLK)
    other = pl.multiple_of((1 - core) * half, BLK)

    def send(src, dst, send_sem, recv_sem, target):
        return pltpu.make_async_remote_copy(
            src_ref=src,
            dst_ref=dst,
            send_sem=send_sem,
            recv_sem=recv_sem,
            device_id={"qblk": target},
            device_id_type=pl.DeviceIdType.MESH,
        )

    barrier = pltpu.get_barrier_semaphore()
    pl.semaphore_signal(
        barrier, inc=1, device_id={"qblk": partner}, device_id_type=pl.DeviceIdType.MESH
    )

    @pl.when(jnp.logical_not(first))
    def _():
        pl.semaphore_signal(
            barrier, inc=1, device_id={"qblk": run - 2}, device_id_type=pl.DeviceIdType.MESH
        )

    @pl.when(jnp.logical_not(last))
    def _():
        pl.semaphore_signal(
            barrier, inc=1, device_id={"qblk": run + 2}, device_id_type=pl.DeviceIdType.MESH
        )

    pl.semaphore_wait(barrier, 1 + jnp.where(first, 0, 1) + jnp.where(last, 0, 1))

    swap = send(own_ref.at[pl.ds(other, half)], inbox_ref, swap_sems.at[0], swap_sems.at[1], partner)
    swap.start()
    swap.wait()

    def passed(piece):
        part = total_ref.at[pl.ds(pl.multiple_of(mine + piece * rows, 16), rows)]
        return send(
            part, carry_ref.at[pl.ds(piece * rows, rows)], down_sems.at[piece],
            arrive_sems.at[piece], run + 2,
        )

    def given(piece):
        part = total_ref.at[pl.ds(pl.multiple_of(mine + piece * rows, 16), rows)]
        return send(part, part, give_sems.at[piece], take_sems.at[piece], partner)

    def taken(piece):
        part = total_ref.at[pl.ds(pl.multiple_of(other + piece * rows, 16), rows)]
        return send(part, part, give_sems.at[piece], take_sems.at[piece], partner)

    for piece in range(pieces):
        span = pl.ds(piece * rows, rows)
        place = pl.ds(pl.multiple_of(mine + piece * rows, 16), rows)
        total_ref[place, :] = own_ref[place, :] + inbox_ref[span, :]

        @pl.when(jnp.logical_not(first))
        def _():
            passed(piece).wait_recv()
            total_ref[place, :] = total_ref[place, :] + carry_ref[span, :]

        @pl.when(jnp.logical_not(last))
        def _():
            passed(piece).start()

        given(piece).start()

    for piece in range(pieces):
        taken(piece).wait_recv()
        given(piece).wait_send()

        @pl.when(jnp.logical_not(last))
        def _():
            passed(piece).wait_send()

    out_ref[...] = total_ref[...]


def sum_up_to_here(own):
    rows, width = own.shape
    pieces = 4
    if lax.axis_size("qblk") % 2 or rows % (2 * pieces * 16):
        return lax.psum(own, "qblk")
    return pl.pallas_call(
        functools.partial(chain_kernel, pieces),
        out_shape=jax.ShapeDtypeStruct(own.shape, own.dtype),
        in_specs=[pl.BlockSpec(memory_space=pltpu.VMEM)],
        out_specs=pl.BlockSpec(memory_space=pltpu.VMEM),
        scratch_shapes=[
            pltpu.VMEM((rows, width), own.dtype),
            pltpu.VMEM((rows // 2, width), own.dtype),
            pltpu.VMEM((rows // 2, width), own.dtype),
            pltpu.SemaphoreType.DMA((2,)),
            pltpu.SemaphoreType.DMA((pieces,)),
            pltpu.SemaphoreType.DMA((pieces,)),
            pltpu.SemaphoreType.DMA((pieces,)),
            pltpu.SemaphoreType.DMA((pieces,)),
        ],
        compiler_params=pltpu.CompilerParams(
            collective_id=0, has_side_effects=True, vmem_limit_bytes=VMEM_LIMIT // 2
        ),
        cost_estimate=pl.CostEstimate(flops=0, bytes_accessed=64 * own.size, transcendentals=0),
        name="sum_up_to_here",
    )(own)


def attend_kernel(
    group,
    kv_heads,
    slash_ref,
    odd_ref,
    q_ref,
    two_ref,
    low_ref,
    high_ref,
    own_ref,
    vert_ref,
    bias_ref,
    out_ref,
    key_ref,
    value_ref,
):
    head = pl.program_id(0)
    slash_count = slash_ref.shape[1]
    rows = q_ref.shape[0]
    blocks = rows // BLK
    front = 2 * blocks

    def load_run(run, ref, kv):
        first = run * rows
        value_ref[first : first + rows, :] = ref[:, (kv_heads + kv) * HD : (kv_heads + kv + 1) * HD]

        def turn(block, carry):
            piece = ref[pl.ds(pl.multiple_of(block * BLK, BLK), BLK), kv * HD : (kv + 1) * HD]
            key_ref[run * blocks + block] = jnp.concatenate([piece, piece], 0).T
            return carry

        lax.fori_loop(0, blocks, turn, 0, unroll=4)

    for kv in range(kv_heads):

        @pl.when(head == kv * group)
        def _():
            load_run(0, two_ref, kv)
            load_run(2, own_ref, kv)

        @pl.when(jnp.logical_and(head == kv * group, odd_ref[0] == 1))
        def _():
            load_run(1, low_ref, kv)

        @pl.when(jnp.logical_and(head == kv * group, odd_ref[0] == 0))
        def _():
            load_run(1, high_ref, kv)

    left = lax.broadcasted_iota(jnp.int32, (HD, 2 * BLK), 1) < BLK
    if (1 + slash_ref.shape[1]) % 2:
        first_vert = vert_ref[:BLK, :HD]
        lead_keys = [jnp.concatenate([first_vert, first_vert], 0).T]
    else:
        lead_keys = []
    scale = HD ** (-0.5) * math.log2(math.e)
    row_ids = lax.broadcasted_iota(jnp.int32, (BLK, 2 * BLK), 0)
    col_ids = lax.broadcasted_iota(jnp.int32, (BLK, 2 * BLK), 1)
    hidden = jnp.logical_and(col_ids < BLK, col_ids > row_ids)
    causal = jnp.where(hidden, MASKED, 0.0).astype(jnp.float32)
    offsets = [0] + [slash_ref[head, slot] for slot in range(slash_count)]
    lead = (1 + slash_count) % 2 * BLK
    split = (1 + slash_count) * BLK + lead
    together = 4 if blocks % 4 == 0 else 1

    def one_group(step, carry):
        base = pl.multiple_of(step * together * BLK, BLK)
        shared = lax.dot_general(
            q_ref[pl.ds(base, together * BLK), :],
            vert_ref[lead:, :HD],
            (((1,), (1,)), ((), ())),
            preferred_element_type=jnp.float32,
        )
        sums, totals, shared_weights = [], [], []
        for part in range(together):
            block = step * together + part
            row = pl.multiple_of(block * BLK, BLK)
            starts = [pl.multiple_of((front + block - offset) * BLK, BLK) for offset in offsets]

            halves = [key_ref[front + block - offset] for offset in offsets] + lead_keys
            keys = [
                jnp.where(left, halves[pair], halves[pair + 1])
                for pair in range(0, len(halves), 2)
            ]
            values = [value_ref[pl.ds(start, BLK), :] for start in starts]
            if lead:
                values.append(vert_ref[:lead, HD:])
            scores = jnp.dot(
                q_ref[pl.ds(row, BLK), :],
                jnp.concatenate(keys, 1),
                preferred_element_type=jnp.float32,
            )
            scores = scores * scale + bias_ref[0, pl.ds(block, 1), :split]
            scores = jnp.concatenate([scores[:, : 2 * BLK] + causal, scores[:, 2 * BLK :]], 1)
            vert_scores = shared[part * BLK : (part + 1) * BLK] * scale
            vert_scores = vert_scores + bias_ref[0, pl.ds(block, 1), split:]
            row_max = jnp.maximum(
                jnp.max(scores, axis=1, keepdims=True),
                jnp.max(vert_scores, axis=1, keepdims=True),
            )
            weights = jnp.exp2(scores - row_max)
            vert_weights = jnp.exp2(vert_scores - row_max)
            totals.append(
                jnp.sum(weights, axis=1, keepdims=True)
                + jnp.sum(vert_weights, axis=1, keepdims=True)
            )
            shared_weights.append(vert_weights.astype(jnp.bfloat16))
            sums.append(
                jnp.dot(
                    weights.astype(jnp.bfloat16),
                    jnp.concatenate(values, 0),
                    preferred_element_type=jnp.float32,
                )
            )
        summed = jnp.dot(
            jnp.concatenate(shared_weights, 0),
            vert_ref[lead:, HD:],
            preferred_element_type=jnp.float32,
        )
        summed = summed + jnp.concatenate(sums, 0)
        out_ref[pl.ds(base, together * BLK), :] = (
            summed / jnp.concatenate(totals, 0)
        ).astype(out_ref.dtype)
        return carry

    lax.fori_loop(0, blocks // together, one_group, 0, unroll=2)


def attend(queries, two_back, low, high, own, odd, vertical, slash, bias, group, kv_heads):
    rows = queries.shape[0]
    q_heads, blocks, width = bias.shape
    vert_rows = vertical.shape[0] // q_heads
    whole = pl.BlockSpec(own.shape, lambda h, s, o: (0, 0))
    return pl.pallas_call(
        functools.partial(attend_kernel, group, kv_heads),
        out_shape=jax.ShapeDtypeStruct((rows, q_heads * HD), queries.dtype),
        grid_spec=pltpu.PrefetchScalarGridSpec(
            num_scalar_prefetch=2,
            grid=(q_heads,),
            in_specs=[
                pl.BlockSpec((rows, HD), lambda h, s, o: (0, h)),
                whole,
                whole,
                whole,
                whole,
                pl.BlockSpec((vert_rows, 2 * HD), lambda h, s, o: (h, 0)),
                pl.BlockSpec((1, blocks, width), lambda h, s, o: (h, 0, 0)),
            ],
            out_specs=pl.BlockSpec((rows, HD), lambda h, s, o: (0, h)),
            scratch_shapes=[
                pltpu.VMEM((3 * blocks, HD, 2 * BLK), queries.dtype),
                pltpu.VMEM((3 * rows, HD), queries.dtype),
            ],
        ),
        compiler_params=pltpu.CompilerParams(
            dimension_semantics=("arbitrary",), vmem_limit_bytes=VMEM_LIMIT
        ),
        cost_estimate=pl.CostEstimate(
            flops=4 * q_heads * rows * width * HD,
            bytes_accessed=4 * q_heads * blocks * width * HD,
            transcendentals=q_heads * rows * width,
        ),
        name="attend",
    )(slash, odd, queries, two_back, low, high, own, vertical, bias)


def per_device(queries, key_states, value_states, vertical_blocks, slash_offsets):
    head_count = lax.axis_size("head")
    head_index = lax.axis_index("head")
    run_count = lax.axis_size("qblk")
    block_index = lax.axis_index("qblk")
    rows_in = queries.shape[0]
    q_heads = H // head_count
    copies = max(1, head_count // KVH)
    kv_heads = KVH * copies // head_count
    group = q_heads // kv_heads

    def by_head(states):
        split = states.reshape(rows_in, KVH, HD)
        if copies > 1:
            split = jnp.repeat(split, copies, axis=1)
        return split.reshape(rows_in, head_count, kv_heads * HD)

    kv_pair = jnp.concatenate([by_head(key_states), by_head(value_states)], axis=2)
    kv_pair = kv_pair.reshape(rows_in, head_count * 2 * kv_heads * HD)
    kv_local = lax.all_to_all(kv_pair, "head", split_axis=1, concat_axis=0, tiled=True)
    row_count = kv_local.shape[0]
    blocks = row_count // BLK
    vert_mine = lax.dynamic_slice_in_dim(vertical_blocks, head_index * q_heads, q_heads, 0)
    slash_mine = lax.dynamic_slice_in_dim(slash_offsets, head_index * q_heads, q_heads, 0)
    first_block = block_index * blocks
    own_vertical = pick_vertical(kv_local, vert_mine - first_block, group, kv_heads)
    own_vertical, vert_mine = lax.optimization_barrier((own_vertical, vert_mine))
    vertical = sum_up_to_here(own_vertical)
    odd = lax.rem(block_index, 2).astype(jnp.int32).reshape(1)

    block_ids = first_block + jnp.arange(blocks, dtype=jnp.int32)
    slash_ok = block_ids[None, :, None] - slash_mine[:, None, :] >= 0
    block_gap = block_ids[None, :, None] - vert_mine[:, None, :]
    slash_hit = jnp.any(block_gap[:, :, :, None] == slash_mine[:, None, None, :], axis=3)
    vert_ok = (block_gap > 0) & jnp.logical_not(slash_hit)
    allowed = jnp.concatenate([jnp.ones((q_heads, blocks, 1), bool), slash_ok, vert_ok], axis=2)
    bias = jnp.where(allowed, 0.0, MASKED).astype(jnp.float32)
    bias = jnp.broadcast_to(bias[:, :, :, None], bias.shape + (BLK,))
    bias = bias.reshape(q_heads, blocks, -1)

    upward = [(run, run + 1) for run in range(0, run_count - 1, 2)]
    downward = [(run + 1, run) for run in range(0, run_count - 1, 2)]
    two_back = from_behind(kv_local, "qblk", 2)
    low = lax.ppermute(kv_local, "qblk", upward)
    high = lax.ppermute(two_back, "qblk", downward)
    q_local = lax.all_to_all(queries, "head", split_axis=1, concat_axis=0, tiled=True)
    attended = attend(
        q_local,
        two_back,
        low,
        high,
        kv_local,
        odd,
        vertical,
        slash_mine,
        bias,
        group,
        kv_heads,
    )
    return lax.all_to_all(attended, "head", split_axis=0, concat_axis=1, tiled=True)


def solution(mesh):
    return jax.shard_map(
        per_device,
        mesh=mesh,
        in_specs=(
            P(("qblk", "head"), None),
            P(("qblk", "head"), None),
            P(("qblk", "head"), None),
            P(),
            P(),
        ),
        out_specs=P(("qblk", "head"), None),
        check_vma=False,
    )
```

```python
import functools
import math

import jax
import jax.numpy as jnp
from jax import lax
from jax.experimental import pallas as pl
from jax.experimental.pallas import tpu as pltpu
from jax.sharding import PartitionSpec as P

H = 32
KVH = 8
HD = 128
BLK = 64
MASKED = -1e30
VMEM_LIMIT = 48 * 1024 * 1024


def from_behind(value, axis, steps):
    count = lax.axis_size(axis)
    leading, last = (max(0, -steps), min(count, count - steps))
    return lax.ppermute(value, axis, [(source, source + steps) for source in range(leading, last)])


def pick_kernel(group, kv_heads, vert_count, offset_ref, kv_ref, out_ref):
    blocks = kv_ref.shape[0] // BLK
    q_heads = out_ref.shape[0] // (vert_count * BLK)
    for head in range(q_heads):
        k_col = (head // group) * HD
        v_col = (kv_heads + head // group) * HD
        for slot in range(vert_count):
            offset = offset_ref[head * vert_count + slot]
            inside = jnp.logical_and(offset >= 0, offset < blocks)
            start = pl.multiple_of(jnp.clip(offset, 0, blocks - 1) * BLK, BLK)
            row = (head * vert_count + slot) * BLK
            for place, col in ((0, k_col), (HD, v_col)):
                piece = kv_ref[pl.ds(start, BLK), col : col + HD]
                out_ref[row : row + BLK, place : place + HD] = jnp.where(
                    inside, piece, jnp.zeros_like(piece)
                )


def pick_vertical(kv_local, offsets, group, kv_heads):
    q_heads, vert_count = offsets.shape
    return pl.pallas_call(
        functools.partial(pick_kernel, group, kv_heads, vert_count),
        out_shape=jax.ShapeDtypeStruct((q_heads * vert_count * BLK, 2 * HD), kv_local.dtype),
        in_specs=[
            pl.BlockSpec(memory_space=pltpu.SMEM),
            pl.BlockSpec(memory_space=pltpu.VMEM),
        ],
        out_specs=pl.BlockSpec(memory_space=pltpu.VMEM),
        compiler_params=pltpu.CompilerParams(vmem_limit_bytes=VMEM_LIMIT),
        name="pick_vertical",
    )(offsets.reshape(-1), kv_local)


def chain_kernel(
    pieces,
    own_ref,
    out_ref,
    total_ref,
    inbox_ref,
    carry_ref,
    swap_sems,
    down_sems,
    arrive_sems,
    give_sems,
    take_sems,
):
    run = lax.axis_index("qblk")
    runs = lax.axis_size("qblk")
    core = lax.rem(run, 2)
    partner = run + 1 - 2 * core
    first = run < 2
    last = run >= runs - 2
    half = own_ref.shape[0] // 2
    rows = half // pieces
    mine = pl.multiple_of(core * half, BLK)
    other = pl.multiple_of((1 - core) * half, BLK)

    def send(src, dst, send_sem, recv_sem, target):
        return pltpu.make_async_remote_copy(
            src_ref=src,
            dst_ref=dst,
            send_sem=send_sem,
            recv_sem=recv_sem,
            device_id={"qblk": target},
            device_id_type=pl.DeviceIdType.MESH,
        )

    barrier = pltpu.get_barrier_semaphore()
    pl.semaphore_signal(
        barrier, inc=1, device_id={"qblk": partner}, device_id_type=pl.DeviceIdType.MESH
    )

    @pl.when(jnp.logical_not(first))
    def _():
        pl.semaphore_signal(
            barrier, inc=1, device_id={"qblk": run - 2}, device_id_type=pl.DeviceIdType.MESH
        )

    @pl.when(jnp.logical_not(last))
    def _():
        pl.semaphore_signal(
            barrier, inc=1, device_id={"qblk": run + 2}, device_id_type=pl.DeviceIdType.MESH
        )

    pl.semaphore_wait(barrier, 1 + jnp.where(first, 0, 1) + jnp.where(last, 0, 1))

    swap = send(own_ref.at[pl.ds(other, half)], inbox_ref, swap_sems.at[0], swap_sems.at[1], partner)
    swap.start()
    swap.wait()

    def passed(piece):
        part = total_ref.at[pl.ds(pl.multiple_of(mine + piece * rows, 16), rows)]
        return send(
            part, carry_ref.at[pl.ds(piece * rows, rows)], down_sems.at[piece],
            arrive_sems.at[piece], run + 2,
        )

    def given(piece):
        part = total_ref.at[pl.ds(pl.multiple_of(mine + piece * rows, 16), rows)]
        return send(part, part, give_sems.at[piece], take_sems.at[piece], partner)

    def taken(piece):
        part = total_ref.at[pl.ds(pl.multiple_of(other + piece * rows, 16), rows)]
        return send(part, part, give_sems.at[piece], take_sems.at[piece], partner)

    for piece in range(pieces):
        span = pl.ds(piece * rows, rows)
        place = pl.ds(pl.multiple_of(mine + piece * rows, 16), rows)
        total_ref[place, :] = own_ref[place, :] + inbox_ref[span, :]

        @pl.when(jnp.logical_not(first))
        def _():
            passed(piece).wait_recv()
            total_ref[place, :] = total_ref[place, :] + carry_ref[span, :]

        @pl.when(jnp.logical_not(last))
        def _():
            passed(piece).start()

        given(piece).start()

    for piece in range(pieces):
        taken(piece).wait_recv()
        given(piece).wait_send()

        @pl.when(jnp.logical_not(last))
        def _():
            passed(piece).wait_send()

    out_ref[...] = total_ref[...]


def sum_up_to_here(own):
    rows, width = own.shape
    pieces = 4
    if lax.axis_size("qblk") % 2 or rows % (2 * pieces * 16):
        return lax.psum(own, "qblk")
    return pl.pallas_call(
        functools.partial(chain_kernel, pieces),
        out_shape=jax.ShapeDtypeStruct(own.shape, own.dtype),
        in_specs=[pl.BlockSpec(memory_space=pltpu.VMEM)],
        out_specs=pl.BlockSpec(memory_space=pltpu.VMEM),
        scratch_shapes=[
            pltpu.VMEM((rows, width), own.dtype),
            pltpu.VMEM((rows // 2, width), own.dtype),
            pltpu.VMEM((rows // 2, width), own.dtype),
            pltpu.SemaphoreType.DMA((2,)),
            pltpu.SemaphoreType.DMA((pieces,)),
            pltpu.SemaphoreType.DMA((pieces,)),
            pltpu.SemaphoreType.DMA((pieces,)),
            pltpu.SemaphoreType.DMA((pieces,)),
        ],
        compiler_params=pltpu.CompilerParams(
            collective_id=0, has_side_effects=True, vmem_limit_bytes=VMEM_LIMIT // 2
        ),
        cost_estimate=pl.CostEstimate(flops=0, bytes_accessed=64 * own.size, transcendentals=0),
        name="sum_up_to_here",
    )(own)


def attend_kernel(
    kv,
    kv_heads,
    slash_ref,
    odd_ref,
    q_ref,
    two_ref,
    low_ref,
    high_ref,
    own_ref,
    vert_ref,
    bias_ref,
    out_ref,
    key_ref,
    value_ref,
):
    head = pl.program_id(0)
    slash_count = slash_ref.shape[1]
    rows = q_ref.shape[0]
    blocks = rows // BLK
    front = 2 * blocks

    def load_run(run, ref, kv):
        first = run * rows
        value_ref[first : first + rows, :] = ref[:, (kv_heads + kv) * HD : (kv_heads + kv + 1) * HD]

        def turn(block, carry):
            piece = ref[pl.ds(pl.multiple_of(block * BLK, BLK), BLK), kv * HD : (kv + 1) * HD]
            key_ref[run * blocks + block] = jnp.concatenate([piece, piece], 0).T
            return carry

        lax.fori_loop(0, blocks, turn, 0, unroll=4)

    @pl.when(head == 0)
    def _():
        load_run(0, two_ref, kv)
        load_run(2, own_ref, kv)

    @pl.when(jnp.logical_and(head == 0, odd_ref[0] == 1))
    def _():
        load_run(1, low_ref, kv)

    @pl.when(jnp.logical_and(head == 0, odd_ref[0] == 0))
    def _():
        load_run(1, high_ref, kv)

    left = lax.broadcasted_iota(jnp.int32, (HD, 2 * BLK), 1) < BLK
    if (1 + slash_ref.shape[1]) % 2:
        first_vert = vert_ref[:BLK, :HD]
        lead_keys = [jnp.concatenate([first_vert, first_vert], 0).T]
    else:
        lead_keys = []
    scale = HD ** (-0.5) * math.log2(math.e)
    row_ids = lax.broadcasted_iota(jnp.int32, (BLK, 2 * BLK), 0)
    col_ids = lax.broadcasted_iota(jnp.int32, (BLK, 2 * BLK), 1)
    hidden = jnp.logical_and(col_ids < BLK, col_ids > row_ids)
    causal = jnp.where(hidden, MASKED, 0.0).astype(jnp.float32)
    offsets = [0] + [slash_ref[head, slot] for slot in range(slash_count)]
    lead = (1 + slash_count) % 2 * BLK
    split = (1 + slash_count) * BLK + lead
    together = 4 if blocks % 4 == 0 else 1

    def one_group(step, carry):
        base = pl.multiple_of(step * together * BLK, BLK)
        shared = lax.dot_general(
            q_ref[pl.ds(base, together * BLK), :],
            vert_ref[lead:, :HD],
            (((1,), (1,)), ((), ())),
            preferred_element_type=jnp.float32,
        )
        sums, totals, shared_weights = [], [], []
        for part in range(together):
            block = step * together + part
            row = pl.multiple_of(block * BLK, BLK)
            starts = [pl.multiple_of((front + block - offset) * BLK, BLK) for offset in offsets]

            halves = [key_ref[front + block - offset] for offset in offsets] + lead_keys
            keys = [
                jnp.where(left, halves[pair], halves[pair + 1])
                for pair in range(0, len(halves), 2)
            ]
            values = [value_ref[pl.ds(start, BLK), :] for start in starts]
            if lead:
                values.append(vert_ref[:lead, HD:])
            scores = jnp.dot(
                q_ref[pl.ds(row, BLK), :],
                jnp.concatenate(keys, 1),
                preferred_element_type=jnp.float32,
            )
            scores = scores * scale + bias_ref[0, pl.ds(block, 1), :split]
            vert_scores = shared[part * BLK : (part + 1) * BLK] * scale
            vert_scores = vert_scores + bias_ref[0, pl.ds(block, 1), split:]
            scores = jnp.concatenate(
                [scores[:, : 2 * BLK] + causal, scores[:, 2 * BLK :], vert_scores], 1
            )
            weights = jnp.exp2(scores - jnp.max(scores, axis=1, keepdims=True))
            totals.append(jnp.sum(weights, axis=1, keepdims=True))
            weights = weights.astype(jnp.bfloat16)
            shared_weights.append(weights[:, split:])
            sums.append(
                jnp.dot(
                    weights[:, :split],
                    jnp.concatenate(values, 0),
                    preferred_element_type=jnp.float32,
                )
            )
        summed = jnp.dot(
            jnp.concatenate(shared_weights, 0),
            vert_ref[lead:, HD:],
            preferred_element_type=jnp.float32,
        )
        summed = summed + jnp.concatenate(sums, 0)
        out_ref[pl.ds(base, together * BLK), :] = (
            summed / jnp.concatenate(totals, 0)
        ).astype(out_ref.dtype)
        return carry

    lax.fori_loop(0, blocks // together, one_group, 0, unroll=2)


def attend(queries, two_back, low, high, own, odd, vertical, slash, bias, kv, kv_heads):
    rows = queries.shape[0]
    _, blocks, width = bias.shape
    q_heads = slash.shape[0]
    vert_rows = vertical.shape[0] // (q_heads * kv_heads)
    base = kv * q_heads
    whole = pl.BlockSpec(own.shape, lambda h, s, o: (0, 0))
    return pl.pallas_call(
        functools.partial(attend_kernel, kv, kv_heads),
        out_shape=jax.ShapeDtypeStruct((rows, q_heads * HD), queries.dtype),
        grid_spec=pltpu.PrefetchScalarGridSpec(
            num_scalar_prefetch=2,
            grid=(q_heads,),
            in_specs=[
                pl.BlockSpec((rows, HD), lambda h, s, o: (0, base + h)),
                whole,
                whole,
                whole,
                whole,
                pl.BlockSpec((vert_rows, 2 * HD), lambda h, s, o: (base + h, 0)),
                pl.BlockSpec((1, blocks, width), lambda h, s, o: (base + h, 0, 0)),
            ],
            out_specs=pl.BlockSpec((rows, HD), lambda h, s, o: (0, h)),
            scratch_shapes=[
                pltpu.VMEM((3 * blocks, HD, 2 * BLK), queries.dtype),
                pltpu.VMEM((3 * rows, HD), queries.dtype),
            ],
        ),
        compiler_params=pltpu.CompilerParams(
            dimension_semantics=("arbitrary",), vmem_limit_bytes=VMEM_LIMIT
        ),
        cost_estimate=pl.CostEstimate(
            flops=4 * q_heads * rows * width * HD,
            bytes_accessed=4 * q_heads * blocks * width * HD,
            transcendentals=q_heads * rows * width,
        ),
        name="attend",
    )(slash, odd, queries, two_back, low, high, own, vertical, bias)


def lay_kernel(*refs):
    out_ref = refs[-1]
    width = refs[0].shape[1]
    for place, part_ref in enumerate(refs[:-1]):
        out_ref[:, place * width : (place + 1) * width] = part_ref[...]


def lay_columns(parts, head_count):
    rows, width = parts[0].shape
    rows = rows // head_count
    return pl.pallas_call(
        lay_kernel,
        out_shape=jax.ShapeDtypeStruct(
            (rows, head_count * len(parts) * width), parts[0].dtype
        ),
        grid=(head_count,),
        in_specs=[pl.BlockSpec((rows, width), lambda peer: (peer, 0)) for _ in parts],
        out_specs=pl.BlockSpec((rows, len(parts) * width), lambda peer: (0, peer)),
        compiler_params=pltpu.CompilerParams(
            dimension_semantics=("arbitrary",), vmem_limit_bytes=VMEM_LIMIT // 2
        ),
        name="lay_columns",
    )(*parts)


def per_device(queries, key_states, value_states, vertical_blocks, slash_offsets):
    head_count = lax.axis_size("head")
    head_index = lax.axis_index("head")
    run_count = lax.axis_size("qblk")
    block_index = lax.axis_index("qblk")
    rows_in = queries.shape[0]
    q_heads = H // head_count
    copies = max(1, head_count // KVH)
    kv_heads = KVH * copies // head_count
    group = q_heads // kv_heads

    def by_head(states):
        split = states.reshape(rows_in, KVH, HD)
        if copies > 1:
            split = jnp.repeat(split, copies, axis=1)
        return split.reshape(rows_in, head_count, kv_heads * HD)

    kv_pair = jnp.concatenate([by_head(key_states), by_head(value_states)], axis=2)
    kv_pair = kv_pair.reshape(rows_in, head_count * 2 * kv_heads * HD)
    kv_local = lax.all_to_all(kv_pair, "head", split_axis=1, concat_axis=0, tiled=True)
    row_count = kv_local.shape[0]
    blocks = row_count // BLK
    vert_mine = lax.dynamic_slice_in_dim(vertical_blocks, head_index * q_heads, q_heads, 0)
    slash_mine = lax.dynamic_slice_in_dim(slash_offsets, head_index * q_heads, q_heads, 0)
    first_block = block_index * blocks
    own_vertical = pick_vertical(kv_local, vert_mine - first_block, group, kv_heads)
    own_vertical, vert_mine = lax.optimization_barrier((own_vertical, vert_mine))
    vertical = sum_up_to_here(own_vertical)
    odd = lax.rem(block_index, 2).astype(jnp.int32).reshape(1)

    block_ids = first_block + jnp.arange(blocks, dtype=jnp.int32)
    slash_ok = block_ids[None, :, None] - slash_mine[:, None, :] >= 0
    block_gap = block_ids[None, :, None] - vert_mine[:, None, :]
    slash_hit = jnp.any(block_gap[:, :, :, None] == slash_mine[:, None, None, :], axis=3)
    vert_ok = (block_gap > 0) & jnp.logical_not(slash_hit)
    allowed = jnp.concatenate([jnp.ones((q_heads, blocks, 1), bool), slash_ok, vert_ok], axis=2)
    bias = jnp.where(allowed, 0.0, MASKED).astype(jnp.float32)
    bias = jnp.broadcast_to(bias[:, :, :, None], bias.shape + (BLK,))
    bias = bias.reshape(q_heads, blocks, -1)

    upward = [(run, run + 1) for run in range(0, run_count - 1, 2)]
    downward = [(run + 1, run) for run in range(0, run_count - 1, 2)]
    two_back = from_behind(kv_local, "qblk", 2)
    low = lax.ppermute(kv_local, "qblk", upward)
    two_back, vertical, bias = lax.optimization_barrier((two_back, vertical, bias))
    high = lax.ppermute(two_back, "qblk", downward)
    q_local = lax.all_to_all(queries, "head", split_axis=1, concat_axis=0, tiled=True)
    parts = []
    for kv in range(kv_heads):
        heads = slice(kv * group, (kv + 1) * group)
        attended = attend(
            q_local,
            two_back,
            low,
            high,
            kv_local,
            odd,
            vertical,
            slash_mine[heads],
            bias,
            kv,
            kv_heads,
        )
        parts.append(lax.all_to_all(attended, "head", split_axis=0, concat_axis=0, tiled=True))
    return lay_columns(parts, head_count)


def solution(mesh):
    return jax.shard_map(
        per_device,
        mesh=mesh,
        in_specs=(
            P(("qblk", "head"), None),
            P(("qblk", "head"), None),
            P(("qblk", "head"), None),
            P(),
            P(),
        ),
        out_specs=P(("qblk", "head"), None),
        check_vma=False,
    )
```

```python
import functools
import math

import jax
import jax.numpy as jnp
from jax import lax
from jax.experimental import pallas as pl
from jax.experimental.pallas import tpu as pltpu
from jax.sharding import PartitionSpec as P

H = 32
KVH = 8
HD = 128
BLK = 64
MASKED = -1e30
VMEM_LIMIT = 48 * 1024 * 1024


def from_behind(value, axis, steps):
    count = lax.axis_size(axis)
    leading, last = (max(0, -steps), min(count, count - steps))
    return lax.ppermute(value, axis, [(source, source + steps) for source in range(leading, last)])


def pick_kernel(group, kv_heads, vert_count, offset_ref, kv_ref, out_ref):
    blocks = kv_ref.shape[0] // BLK
    q_heads = out_ref.shape[0] // (vert_count * BLK)
    for head in range(q_heads):
        k_col = (head // group) * HD
        v_col = (kv_heads + head // group) * HD
        for slot in range(vert_count):
            offset = offset_ref[head * vert_count + slot]
            inside = jnp.logical_and(offset >= 0, offset < blocks)
            start = pl.multiple_of(jnp.clip(offset, 0, blocks - 1) * BLK, BLK)
            row = (head * vert_count + slot) * BLK
            for place, col in ((0, k_col), (HD, v_col)):
                piece = kv_ref[pl.ds(start, BLK), col : col + HD]
                out_ref[row : row + BLK, place : place + HD] = jnp.where(
                    inside, piece, jnp.zeros_like(piece)
                )


def pick_vertical(kv_local, offsets, group, kv_heads):
    q_heads, vert_count = offsets.shape
    return pl.pallas_call(
        functools.partial(pick_kernel, group, kv_heads, vert_count),
        out_shape=jax.ShapeDtypeStruct((q_heads * vert_count * BLK, 2 * HD), kv_local.dtype),
        in_specs=[
            pl.BlockSpec(memory_space=pltpu.SMEM),
            pl.BlockSpec(memory_space=pltpu.VMEM),
        ],
        out_specs=pl.BlockSpec(memory_space=pltpu.VMEM),
        compiler_params=pltpu.CompilerParams(vmem_limit_bytes=VMEM_LIMIT),
        name="pick_vertical",
    )(offsets.reshape(-1), kv_local)


def chain_kernel(
    pieces,
    own_ref,
    out_ref,
    total_ref,
    inbox_ref,
    carry_ref,
    swap_sems,
    down_sems,
    arrive_sems,
    give_sems,
    take_sems,
):
    run = lax.axis_index("qblk")
    runs = lax.axis_size("qblk")
    core = lax.rem(run, 2)
    partner = run + 1 - 2 * core
    first = run < 2
    last = run >= runs - 2
    half = own_ref.shape[0] // 2
    rows = half // pieces
    mine = pl.multiple_of(core * half, BLK)
    other = pl.multiple_of((1 - core) * half, BLK)

    def send(src, dst, send_sem, recv_sem, target):
        return pltpu.make_async_remote_copy(
            src_ref=src,
            dst_ref=dst,
            send_sem=send_sem,
            recv_sem=recv_sem,
            device_id={"qblk": target},
            device_id_type=pl.DeviceIdType.MESH,
        )

    barrier = pltpu.get_barrier_semaphore()
    pl.semaphore_signal(
        barrier, inc=1, device_id={"qblk": partner}, device_id_type=pl.DeviceIdType.MESH
    )

    @pl.when(jnp.logical_not(first))
    def _():
        pl.semaphore_signal(
            barrier, inc=1, device_id={"qblk": run - 2}, device_id_type=pl.DeviceIdType.MESH
        )

    @pl.when(jnp.logical_not(last))
    def _():
        pl.semaphore_signal(
            barrier, inc=1, device_id={"qblk": run + 2}, device_id_type=pl.DeviceIdType.MESH
        )

    pl.semaphore_wait(barrier, 1 + jnp.where(first, 0, 1) + jnp.where(last, 0, 1))

    swap = send(own_ref.at[pl.ds(other, half)], inbox_ref, swap_sems.at[0], swap_sems.at[1], partner)
    swap.start()
    swap.wait()

    def passed(piece):
        part = total_ref.at[pl.ds(pl.multiple_of(mine + piece * rows, 16), rows)]
        return send(
            part, carry_ref.at[pl.ds(piece * rows, rows)], down_sems.at[piece],
            arrive_sems.at[piece], run + 2,
        )

    def given(piece):
        part = total_ref.at[pl.ds(pl.multiple_of(mine + piece * rows, 16), rows)]
        return send(part, part, give_sems.at[piece], take_sems.at[piece], partner)

    def taken(piece):
        part = total_ref.at[pl.ds(pl.multiple_of(other + piece * rows, 16), rows)]
        return send(part, part, give_sems.at[piece], take_sems.at[piece], partner)

    for piece in range(pieces):
        span = pl.ds(piece * rows, rows)
        place = pl.ds(pl.multiple_of(mine + piece * rows, 16), rows)
        total_ref[place, :] = own_ref[place, :] + inbox_ref[span, :]

        @pl.when(jnp.logical_not(first))
        def _():
            passed(piece).wait_recv()
            total_ref[place, :] = total_ref[place, :] + carry_ref[span, :]

        @pl.when(jnp.logical_not(last))
        def _():
            passed(piece).start()

        given(piece).start()

    for piece in range(pieces):
        taken(piece).wait_recv()
        given(piece).wait_send()

        @pl.when(jnp.logical_not(last))
        def _():
            passed(piece).wait_send()

    out_ref[...] = total_ref[...]


def sum_up_to_here(own):
    rows, width = own.shape
    pieces = 4
    if lax.axis_size("qblk") % 2 or rows % (2 * pieces * 16):
        return lax.psum(own, "qblk")
    return pl.pallas_call(
        functools.partial(chain_kernel, pieces),
        out_shape=jax.ShapeDtypeStruct(own.shape, own.dtype),
        in_specs=[pl.BlockSpec(memory_space=pltpu.VMEM)],
        out_specs=pl.BlockSpec(memory_space=pltpu.VMEM),
        scratch_shapes=[
            pltpu.VMEM((rows, width), own.dtype),
            pltpu.VMEM((rows // 2, width), own.dtype),
            pltpu.VMEM((rows // 2, width), own.dtype),
            pltpu.SemaphoreType.DMA((2,)),
            pltpu.SemaphoreType.DMA((pieces,)),
            pltpu.SemaphoreType.DMA((pieces,)),
            pltpu.SemaphoreType.DMA((pieces,)),
            pltpu.SemaphoreType.DMA((pieces,)),
        ],
        compiler_params=pltpu.CompilerParams(
            collective_id=0, has_side_effects=True, vmem_limit_bytes=VMEM_LIMIT // 2
        ),
        cost_estimate=pl.CostEstimate(flops=0, bytes_accessed=64 * own.size, transcendentals=0),
        name="sum_up_to_here",
    )(own)


def attend_kernel(
    kv,
    kv_heads,
    slash_ref,
    odd_ref,
    q_ref,
    two_ref,
    low_ref,
    high_ref,
    own_ref,
    vert_ref,
    bias_ref,
    out_ref,
    key_ref,
    value_ref,
):
    head = pl.program_id(0)
    slash_count = slash_ref.shape[1]
    rows = q_ref.shape[0]
    blocks = rows // BLK
    front = 2 * blocks

    def load_run(run, ref, kv):
        first = run * rows
        value_ref[first : first + rows, :] = ref[:, (kv_heads + kv) * HD : (kv_heads + kv + 1) * HD]

        def turn(block, carry):
            piece = ref[pl.ds(pl.multiple_of(block * BLK, BLK), BLK), kv * HD : (kv + 1) * HD]
            key_ref[run * blocks + block] = jnp.concatenate([piece, piece], 0).T
            return carry

        lax.fori_loop(0, blocks, turn, 0, unroll=4)

    @pl.when(head == 0)
    def _():
        load_run(0, two_ref, kv)
        load_run(2, own_ref, kv)

    @pl.when(jnp.logical_and(head == 0, odd_ref[0] == 1))
    def _():
        load_run(1, low_ref, kv)

    @pl.when(jnp.logical_and(head == 0, odd_ref[0] == 0))
    def _():
        load_run(1, high_ref, kv)

    left = lax.broadcasted_iota(jnp.int32, (HD, 2 * BLK), 1) < BLK
    if (1 + slash_ref.shape[1]) % 2:
        first_vert = vert_ref[:BLK, :HD]
        lead_keys = [jnp.concatenate([first_vert, first_vert], 0).T]
    else:
        lead_keys = []
    scale = HD ** (-0.5) * math.log2(math.e)
    row_ids = lax.broadcasted_iota(jnp.int32, (BLK, 2 * BLK), 0)
    col_ids = lax.broadcasted_iota(jnp.int32, (BLK, 2 * BLK), 1)
    hidden = jnp.logical_and(col_ids < BLK, col_ids > row_ids)
    causal = jnp.where(hidden, MASKED, 0.0).astype(jnp.float32)
    offsets = [0] + [slash_ref[head, slot] for slot in range(slash_count)]
    lead = (1 + slash_count) % 2 * BLK
    split = (1 + slash_count) * BLK + lead
    together = 4 if blocks % 4 == 0 else 1

    def one_group(step, carry):
        base = pl.multiple_of(step * together * BLK, BLK)
        shared = lax.dot_general(
            q_ref[pl.ds(base, together * BLK), :],
            vert_ref[lead:, :HD],
            (((1,), (1,)), ((), ())),
            preferred_element_type=jnp.float32,
        )
        parts = range(together)
        group_scores, group_values = [], []
        for part in parts:
            block = step * together + part
            row = pl.multiple_of(block * BLK, BLK)
            starts = [pl.multiple_of((front + block - offset) * BLK, BLK) for offset in offsets]
            halves = [key_ref[front + block - offset] for offset in offsets] + lead_keys
            keys = [
                jnp.where(left, halves[pair], halves[pair + 1])
                for pair in range(0, len(halves), 2)
            ]
            values = [value_ref[pl.ds(start, BLK), :] for start in starts]
            if lead:
                values.append(vert_ref[:lead, HD:])
            group_values.append(values)
            group_scores.append(
                jnp.dot(
                    q_ref[pl.ds(row, BLK), :],
                    jnp.concatenate(keys, 1),
                    preferred_element_type=jnp.float32,
                )
            )
        masked, tops, weights = [], [], []
        for part in parts:
            block = step * together + part
            scores = jnp.concatenate(
                [group_scores[part], shared[part * BLK : (part + 1) * BLK]], 1
            )
            scores = scores * scale + bias_ref[0, pl.ds(block, 1), :]
            masked.append(
                jnp.concatenate([scores[:, : 2 * BLK] + causal, scores[:, 2 * BLK :]], 1)
            )
            tops.append(jnp.max(masked[part], axis=1, keepdims=True))
        for part in parts:
            weights.append(jnp.exp2(masked[part] - tops[part]))
        totals = [jnp.sum(weights[part], axis=1, keepdims=True) for part in parts]
        weights = [weights[part].astype(jnp.bfloat16) for part in parts]
        sums = [
            jnp.dot(
                weights[part][:, :split],
                jnp.concatenate(group_values[part], 0),
                preferred_element_type=jnp.float32,
            )
            for part in parts
        ]
        shared_weights = [weights[part][:, split:] for part in parts]
        summed = jnp.dot(
            jnp.concatenate(shared_weights, 0),
            vert_ref[lead:, HD:],
            preferred_element_type=jnp.float32,
        )
        summed = summed + jnp.concatenate(sums, 0)
        out_ref[pl.ds(base, together * BLK), :] = (
            summed / jnp.concatenate(totals, 0)
        ).astype(out_ref.dtype)
        return carry

    lax.fori_loop(0, blocks // together, one_group, 0, unroll=2)


def attend(queries, two_back, low, high, own, odd, vertical, slash, bias, kv, kv_heads):
    rows = queries.shape[0]
    _, blocks, width = bias.shape
    q_heads = slash.shape[0]
    vert_rows = vertical.shape[0] // (q_heads * kv_heads)
    base = kv * q_heads
    whole = pl.BlockSpec(own.shape, lambda h, s, o: (0, 0))
    return pl.pallas_call(
        functools.partial(attend_kernel, kv, kv_heads),
        out_shape=jax.ShapeDtypeStruct((rows, q_heads * HD), queries.dtype),
        grid_spec=pltpu.PrefetchScalarGridSpec(
            num_scalar_prefetch=2,
            grid=(q_heads,),
            in_specs=[
                pl.BlockSpec((rows, HD), lambda h, s, o: (0, base + h)),
                whole,
                whole,
                whole,
                whole,
                pl.BlockSpec((vert_rows, 2 * HD), lambda h, s, o: (base + h, 0)),
                pl.BlockSpec((1, blocks, width), lambda h, s, o: (base + h, 0, 0)),
            ],
            out_specs=pl.BlockSpec((rows, HD), lambda h, s, o: (0, h)),
            scratch_shapes=[
                pltpu.VMEM((3 * blocks, HD, 2 * BLK), queries.dtype),
                pltpu.VMEM((3 * rows, HD), queries.dtype),
            ],
        ),
        compiler_params=pltpu.CompilerParams(
            dimension_semantics=("arbitrary",), vmem_limit_bytes=VMEM_LIMIT
        ),
        cost_estimate=pl.CostEstimate(
            flops=4 * q_heads * rows * width * HD,
            bytes_accessed=4 * q_heads * blocks * width * HD,
            transcendentals=q_heads * rows * width,
        ),
        name="attend",
    )(slash, odd, queries, two_back, low, high, own, vertical, bias)


def lay_kernel(*refs):
    out_ref = refs[-1]
    width = refs[0].shape[1]
    for place, part_ref in enumerate(refs[:-1]):
        out_ref[:, place * width : (place + 1) * width] = part_ref[...]


def lay_columns(parts, head_count):
    rows, width = parts[0].shape
    rows = rows // head_count
    return pl.pallas_call(
        lay_kernel,
        out_shape=jax.ShapeDtypeStruct(
            (rows, head_count * len(parts) * width), parts[0].dtype
        ),
        grid=(head_count,),
        in_specs=[pl.BlockSpec((rows, width), lambda peer: (peer, 0)) for _ in parts],
        out_specs=pl.BlockSpec((rows, len(parts) * width), lambda peer: (0, peer)),
        compiler_params=pltpu.CompilerParams(
            dimension_semantics=("arbitrary",), vmem_limit_bytes=VMEM_LIMIT // 2
        ),
        name="lay_columns",
    )(*parts)


def per_device(queries, key_states, value_states, vertical_blocks, slash_offsets):
    head_count = lax.axis_size("head")
    head_index = lax.axis_index("head")
    run_count = lax.axis_size("qblk")
    block_index = lax.axis_index("qblk")
    rows_in = queries.shape[0]
    q_heads = H // head_count
    copies = max(1, head_count // KVH)
    kv_heads = KVH * copies // head_count
    group = q_heads // kv_heads

    def by_head(states):
        split = states.reshape(rows_in, KVH, HD)
        if copies > 1:
            split = jnp.repeat(split, copies, axis=1)
        return split.reshape(rows_in, head_count, kv_heads * HD)

    kv_pair = jnp.concatenate([by_head(key_states), by_head(value_states)], axis=2)
    kv_pair = kv_pair.reshape(rows_in, head_count * 2 * kv_heads * HD)
    kv_local = lax.all_to_all(kv_pair, "head", split_axis=1, concat_axis=0, tiled=True)
    row_count = kv_local.shape[0]
    blocks = row_count // BLK
    vert_mine = lax.dynamic_slice_in_dim(vertical_blocks, head_index * q_heads, q_heads, 0)
    slash_mine = lax.dynamic_slice_in_dim(slash_offsets, head_index * q_heads, q_heads, 0)
    first_block = block_index * blocks
    own_vertical = pick_vertical(kv_local, vert_mine - first_block, group, kv_heads)
    own_vertical, vert_mine = lax.optimization_barrier((own_vertical, vert_mine))
    odd = lax.rem(block_index, 2).astype(jnp.int32).reshape(1)

    block_ids = first_block + jnp.arange(blocks, dtype=jnp.int32)
    slash_ok = block_ids[None, :, None] - slash_mine[:, None, :] >= 0
    block_gap = block_ids[None, :, None] - vert_mine[:, None, :]
    slash_hit = jnp.any(block_gap[:, :, :, None] == slash_mine[:, None, None, :], axis=3)
    vert_ok = (block_gap > 0) & jnp.logical_not(slash_hit)
    allowed = jnp.concatenate([jnp.ones((q_heads, blocks, 1), bool), slash_ok, vert_ok], axis=2)
    bias = jnp.where(allowed, 0.0, MASKED).astype(jnp.float32)
    bias = jnp.broadcast_to(bias[:, :, :, None], bias.shape + (BLK,))
    bias = bias.reshape(q_heads, blocks, -1)

    upward = [(run, run + 1) for run in range(0, run_count - 1, 2)]
    downward = [(run + 1, run) for run in range(0, run_count - 1, 2)]
    two_back = from_behind(kv_local, "qblk", 2)
    low = lax.ppermute(kv_local, "qblk", upward)
    own_vertical, bias = lax.optimization_barrier((own_vertical, bias))
    vertical = sum_up_to_here(own_vertical)
    two_back, vertical = lax.optimization_barrier((two_back, vertical))
    high = lax.ppermute(two_back, "qblk", downward)
    q_local = lax.all_to_all(queries, "head", split_axis=1, concat_axis=0, tiled=True)
    parts = []
    for kv in range(kv_heads):
        heads = slice(kv * group, (kv + 1) * group)
        attended = attend(
            q_local,
            two_back,
            low,
            high,
            kv_local,
            odd,
            vertical,
            slash_mine[heads],
            bias,
            kv,
            kv_heads,
        )
        parts.append(lax.all_to_all(attended, "head", split_axis=0, concat_axis=0, tiled=True))
    return lay_columns(parts, head_count)


def solution(mesh):
    return jax.shard_map(
        per_device,
        mesh=mesh,
        in_specs=(
            P(("qblk", "head"), None),
            P(("qblk", "head"), None),
            P(("qblk", "head"), None),
            P(),
            P(),
        ),
        out_specs=P(("qblk", "head"), None),
        check_vma=False,
    )
```

```python
import functools
import math

import jax
import jax.numpy as jnp
from jax import lax
from jax.experimental import pallas as pl
from jax.experimental.pallas import tpu as pltpu
from jax.sharding import PartitionSpec as P

H = 32
KVH = 8
HD = 128
BLK = 64
MASKED = -1e30
VMEM_LIMIT = 48 * 1024 * 1024


def from_behind(value, axis, steps):
    count = lax.axis_size(axis)
    leading, last = (max(0, -steps), min(count, count - steps))
    return lax.ppermute(value, axis, [(source, source + steps) for source in range(leading, last)])


def pick_kernel(group, kv_heads, vert_count, offset_ref, kv_ref, out_ref):
    blocks = kv_ref.shape[0] // BLK
    q_heads = out_ref.shape[0] // (vert_count * BLK)
    for head in range(q_heads):
        k_col = (head // group) * HD
        v_col = (kv_heads + head // group) * HD
        for slot in range(vert_count):
            offset = offset_ref[head * vert_count + slot]
            inside = jnp.logical_and(offset >= 0, offset < blocks)
            start = pl.multiple_of(jnp.clip(offset, 0, blocks - 1) * BLK, BLK)
            row = (head * vert_count + slot) * BLK
            for place, col in ((0, k_col), (HD, v_col)):
                piece = kv_ref[pl.ds(start, BLK), col : col + HD]
                out_ref[row : row + BLK, place : place + HD] = jnp.where(
                    inside, piece, jnp.zeros_like(piece)
                )


def pick_vertical(kv_local, offsets, group, kv_heads):
    q_heads, vert_count = offsets.shape
    return pl.pallas_call(
        functools.partial(pick_kernel, group, kv_heads, vert_count),
        out_shape=jax.ShapeDtypeStruct((q_heads * vert_count * BLK, 2 * HD), kv_local.dtype),
        in_specs=[
            pl.BlockSpec(memory_space=pltpu.SMEM),
            pl.BlockSpec(memory_space=pltpu.VMEM),
        ],
        out_specs=pl.BlockSpec(memory_space=pltpu.VMEM),
        compiler_params=pltpu.CompilerParams(vmem_limit_bytes=VMEM_LIMIT),
        name="pick_vertical",
    )(offsets.reshape(-1), kv_local)


def chain_kernel(
    pieces,
    own_ref,
    out_ref,
    total_ref,
    inbox_ref,
    carry_ref,
    swap_sems,
    down_sems,
    arrive_sems,
    give_sems,
    take_sems,
):
    run = lax.axis_index("qblk")
    runs = lax.axis_size("qblk")
    core = lax.rem(run, 2)
    partner = run + 1 - 2 * core
    first = run < 2
    last = run >= runs - 2
    half = own_ref.shape[0] // 2
    rows = half // pieces
    mine = pl.multiple_of(core * half, BLK)
    other = pl.multiple_of((1 - core) * half, BLK)

    def send(src, dst, send_sem, recv_sem, target):
        return pltpu.make_async_remote_copy(
            src_ref=src,
            dst_ref=dst,
            send_sem=send_sem,
            recv_sem=recv_sem,
            device_id={"qblk": target},
            device_id_type=pl.DeviceIdType.MESH,
        )

    barrier = pltpu.get_barrier_semaphore()
    pl.semaphore_signal(
        barrier, inc=1, device_id={"qblk": partner}, device_id_type=pl.DeviceIdType.MESH
    )

    @pl.when(jnp.logical_not(first))
    def _():
        pl.semaphore_signal(
            barrier, inc=1, device_id={"qblk": run - 2}, device_id_type=pl.DeviceIdType.MESH
        )

    @pl.when(jnp.logical_not(last))
    def _():
        pl.semaphore_signal(
            barrier, inc=1, device_id={"qblk": run + 2}, device_id_type=pl.DeviceIdType.MESH
        )

    pl.semaphore_wait(barrier, 1 + jnp.where(first, 0, 1) + jnp.where(last, 0, 1))

    swap = send(own_ref.at[pl.ds(other, half)], inbox_ref, swap_sems.at[0], swap_sems.at[1], partner)
    swap.start()
    swap.wait()

    def passed(piece):
        part = total_ref.at[pl.ds(pl.multiple_of(mine + piece * rows, 16), rows)]
        return send(
            part, carry_ref.at[pl.ds(piece * rows, rows)], down_sems.at[piece],
            arrive_sems.at[piece], run + 2,
        )

    def given(piece):
        part = total_ref.at[pl.ds(pl.multiple_of(mine + piece * rows, 16), rows)]
        return send(part, part, give_sems.at[piece], take_sems.at[piece], partner)

    def taken(piece):
        part = total_ref.at[pl.ds(pl.multiple_of(other + piece * rows, 16), rows)]
        return send(part, part, give_sems.at[piece], take_sems.at[piece], partner)

    for piece in range(pieces):
        span = pl.ds(piece * rows, rows)
        place = pl.ds(pl.multiple_of(mine + piece * rows, 16), rows)
        total_ref[place, :] = own_ref[place, :] + inbox_ref[span, :]

        @pl.when(jnp.logical_not(first))
        def _():
            passed(piece).wait_recv()
            total_ref[place, :] = total_ref[place, :] + carry_ref[span, :]

        @pl.when(jnp.logical_not(last))
        def _():
            passed(piece).start()

        given(piece).start()

    for piece in range(pieces):
        taken(piece).wait_recv()
        given(piece).wait_send()

        @pl.when(jnp.logical_not(last))
        def _():
            passed(piece).wait_send()

    out_ref[...] = total_ref[...]


def sum_up_to_here(own):
    rows, width = own.shape
    pieces = 4
    if lax.axis_size("qblk") % 2 or rows % (2 * pieces * 16):
        return lax.psum(own, "qblk")
    return pl.pallas_call(
        functools.partial(chain_kernel, pieces),
        out_shape=jax.ShapeDtypeStruct(own.shape, own.dtype),
        in_specs=[pl.BlockSpec(memory_space=pltpu.VMEM)],
        out_specs=pl.BlockSpec(memory_space=pltpu.VMEM),
        scratch_shapes=[
            pltpu.VMEM((rows, width), own.dtype),
            pltpu.VMEM((rows // 2, width), own.dtype),
            pltpu.VMEM((rows // 2, width), own.dtype),
            pltpu.SemaphoreType.DMA((2,)),
            pltpu.SemaphoreType.DMA((pieces,)),
            pltpu.SemaphoreType.DMA((pieces,)),
            pltpu.SemaphoreType.DMA((pieces,)),
            pltpu.SemaphoreType.DMA((pieces,)),
        ],
        compiler_params=pltpu.CompilerParams(
            collective_id=0, has_side_effects=True, vmem_limit_bytes=VMEM_LIMIT // 2
        ),
        cost_estimate=pl.CostEstimate(flops=0, bytes_accessed=64 * own.size, transcendentals=0),
        name="sum_up_to_here",
    )(own)


def attend_kernel(
    kv,
    kv_heads,
    slash_ref,
    odd_ref,
    q_ref,
    two_ref,
    low_ref,
    high_ref,
    own_ref,
    vert_ref,
    bias_ref,
    out_ref,
    key_ref,
    value_ref,
):
    head = pl.program_id(0)
    slash_count = slash_ref.shape[1]
    rows = q_ref.shape[0]
    blocks = rows // BLK
    front = 2 * blocks

    def load_run(run, ref, kv):
        first = run * rows
        value_ref[first : first + rows, :] = ref[:, (kv_heads + kv) * HD : (kv_heads + kv + 1) * HD]

        def turn(block, carry):
            piece = ref[pl.ds(pl.multiple_of(block * BLK, BLK), BLK), kv * HD : (kv + 1) * HD]
            key_ref[run * blocks + block] = jnp.concatenate([piece, piece], 0).T
            return carry

        lax.fori_loop(0, blocks, turn, 0, unroll=4)

    @pl.when(head == 0)
    def _():
        load_run(0, two_ref, kv)
        load_run(2, own_ref, kv)

    @pl.when(jnp.logical_and(head == 0, odd_ref[0] == 1))
    def _():
        load_run(1, low_ref, kv)

    @pl.when(jnp.logical_and(head == 0, odd_ref[0] == 0))
    def _():
        load_run(1, high_ref, kv)

    left = lax.broadcasted_iota(jnp.int32, (HD, 2 * BLK), 1) < BLK
    if (1 + slash_ref.shape[1]) % 2:
        first_vert = vert_ref[:BLK, :HD]
        lead_keys = [jnp.concatenate([first_vert, first_vert], 0).T]
    else:
        lead_keys = []
    scale = HD ** (-0.5) * math.log2(math.e)
    row_ids = lax.broadcasted_iota(jnp.int32, (BLK, 2 * BLK), 0)
    col_ids = lax.broadcasted_iota(jnp.int32, (BLK, 2 * BLK), 1)
    hidden = jnp.logical_and(col_ids < BLK, col_ids > row_ids)
    causal = jnp.where(hidden, MASKED, 0.0).astype(jnp.float32)
    offsets = [0] + [slash_ref[head, slot] for slot in range(slash_count)]
    lead = (1 + slash_count) % 2 * BLK
    split = (1 + slash_count) * BLK + lead
    together = next(count for count in (8, 4, 2, 1) if blocks % count == 0)

    def one_group(step, carry):
        base = pl.multiple_of(step * together * BLK, BLK)
        shared = lax.dot_general(
            q_ref[pl.ds(base, together * BLK), :],
            vert_ref[lead:, :HD],
            (((1,), (1,)), ((), ())),
            preferred_element_type=jnp.float32,
        )
        parts = range(together)
        group_scores, group_values = [], []
        for part in parts:
            block = step * together + part
            row = pl.multiple_of(block * BLK, BLK)
            starts = [pl.multiple_of((front + block - offset) * BLK, BLK) for offset in offsets]
            halves = [key_ref[front + block - offset] for offset in offsets] + lead_keys
            keys = [
                jnp.where(left, halves[pair], halves[pair + 1])
                for pair in range(0, len(halves), 2)
            ]
            values = [value_ref[pl.ds(start, BLK), :] for start in starts]
            if lead:
                values.append(vert_ref[:lead, HD:])
            group_values.append(values)
            group_scores.append(
                jnp.dot(
                    q_ref[pl.ds(row, BLK), :],
                    jnp.concatenate(keys, 1),
                    preferred_element_type=jnp.float32,
                )
            )
        masked, tops, weights = [], [], []
        for part in parts:
            block = step * together + part
            scores = jnp.concatenate(
                [group_scores[part], shared[part * BLK : (part + 1) * BLK]], 1
            )
            scores = scores * scale + bias_ref[0, pl.ds(block, 1), :]
            masked.append(
                jnp.concatenate([scores[:, : 2 * BLK] + causal, scores[:, 2 * BLK :]], 1)
            )
            tops.append(jnp.max(masked[part], axis=1, keepdims=True))
        for part in parts:
            weights.append(jnp.exp2(masked[part] - tops[part]))
        totals = [jnp.sum(weights[part], axis=1, keepdims=True) for part in parts]
        weights = [weights[part].astype(jnp.bfloat16) for part in parts]
        sums = [
            jnp.dot(
                weights[part][:, :split],
                jnp.concatenate(group_values[part], 0),
                preferred_element_type=jnp.float32,
            )
            for part in parts
        ]
        shared_weights = [weights[part][:, split:] for part in parts]
        summed = jnp.dot(
            jnp.concatenate(shared_weights, 0),
            vert_ref[lead:, HD:],
            preferred_element_type=jnp.float32,
        )
        summed = summed + jnp.concatenate(sums, 0)
        out_ref[pl.ds(base, together * BLK), :] = (
            summed / jnp.concatenate(totals, 0)
        ).astype(out_ref.dtype)
        return carry

    lax.fori_loop(0, blocks // together, one_group, 0)


def attend(queries, two_back, low, high, own, odd, vertical, slash, bias, kv, kv_heads):
    rows = queries.shape[0]
    _, blocks, width = bias.shape
    q_heads = slash.shape[0]
    vert_rows = vertical.shape[0] // (q_heads * kv_heads)
    base = kv * q_heads
    whole = pl.BlockSpec(own.shape, lambda h, s, o: (0, 0))
    return pl.pallas_call(
        functools.partial(attend_kernel, kv, kv_heads),
        out_shape=jax.ShapeDtypeStruct((rows, q_heads * HD), queries.dtype),
        grid_spec=pltpu.PrefetchScalarGridSpec(
            num_scalar_prefetch=2,
            grid=(q_heads,),
            in_specs=[
                pl.BlockSpec((rows, HD), lambda h, s, o: (0, base + h)),
                whole,
                whole,
                whole,
                whole,
                pl.BlockSpec((vert_rows, 2 * HD), lambda h, s, o: (base + h, 0)),
                pl.BlockSpec((1, blocks, width), lambda h, s, o: (base + h, 0, 0)),
            ],
            out_specs=pl.BlockSpec((rows, HD), lambda h, s, o: (0, h)),
            scratch_shapes=[
                pltpu.VMEM((3 * blocks, HD, 2 * BLK), queries.dtype),
                pltpu.VMEM((3 * rows, HD), queries.dtype),
            ],
        ),
        compiler_params=pltpu.CompilerParams(
            dimension_semantics=("arbitrary",), vmem_limit_bytes=VMEM_LIMIT
        ),
        cost_estimate=pl.CostEstimate(
            flops=4 * q_heads * rows * width * HD,
            bytes_accessed=4 * q_heads * blocks * width * HD,
            transcendentals=q_heads * rows * width,
        ),
        name="attend",
    )(slash, odd, queries, two_back, low, high, own, vertical, bias)


def lay_kernel(*refs):
    out_ref = refs[-1]
    width = refs[0].shape[1]
    for place, part_ref in enumerate(refs[:-1]):
        out_ref[:, place * width : (place + 1) * width] = part_ref[...]


def lay_columns(parts, head_count):
    rows, width = parts[0].shape
    rows = rows // head_count
    return pl.pallas_call(
        lay_kernel,
        out_shape=jax.ShapeDtypeStruct(
            (rows, head_count * len(parts) * width), parts[0].dtype
        ),
        grid=(head_count,),
        in_specs=[pl.BlockSpec((rows, width), lambda peer: (peer, 0)) for _ in parts],
        out_specs=pl.BlockSpec((rows, len(parts) * width), lambda peer: (0, peer)),
        compiler_params=pltpu.CompilerParams(
            dimension_semantics=("arbitrary",), vmem_limit_bytes=VMEM_LIMIT // 2
        ),
        name="lay_columns",
    )(*parts)


def per_device(queries, key_states, value_states, vertical_blocks, slash_offsets):
    head_count = lax.axis_size("head")
    head_index = lax.axis_index("head")
    run_count = lax.axis_size("qblk")
    block_index = lax.axis_index("qblk")
    rows_in = queries.shape[0]
    q_heads = H // head_count
    copies = max(1, head_count // KVH)
    kv_heads = KVH * copies // head_count
    group = q_heads // kv_heads

    def by_head(states):
        split = states.reshape(rows_in, KVH, HD)
        if copies > 1:
            split = jnp.repeat(split, copies, axis=1)
        return split.reshape(rows_in, head_count, kv_heads * HD)

    kv_pair = jnp.concatenate([by_head(key_states), by_head(value_states)], axis=2)
    kv_pair = kv_pair.reshape(rows_in, head_count * 2 * kv_heads * HD)
    kv_local = lax.all_to_all(kv_pair, "head", split_axis=1, concat_axis=0, tiled=True)
    row_count = kv_local.shape[0]
    blocks = row_count // BLK
    vert_mine = lax.dynamic_slice_in_dim(vertical_blocks, head_index * q_heads, q_heads, 0)
    slash_mine = lax.dynamic_slice_in_dim(slash_offsets, head_index * q_heads, q_heads, 0)
    first_block = block_index * blocks
    own_vertical = pick_vertical(kv_local, vert_mine - first_block, group, kv_heads)
    own_vertical, vert_mine = lax.optimization_barrier((own_vertical, vert_mine))
    odd = lax.rem(block_index, 2).astype(jnp.int32).reshape(1)

    block_ids = first_block + jnp.arange(blocks, dtype=jnp.int32)
    slash_ok = block_ids[None, :, None] - slash_mine[:, None, :] >= 0
    block_gap = block_ids[None, :, None] - vert_mine[:, None, :]
    slash_hit = jnp.any(block_gap[:, :, :, None] == slash_mine[:, None, None, :], axis=3)
    vert_ok = (block_gap > 0) & jnp.logical_not(slash_hit)
    allowed = jnp.concatenate([jnp.ones((q_heads, blocks, 1), bool), slash_ok, vert_ok], axis=2)
    bias = jnp.where(allowed, 0.0, MASKED).astype(jnp.float32)
    bias = jnp.broadcast_to(bias[:, :, :, None], bias.shape + (BLK,))
    bias = bias.reshape(q_heads, blocks, -1)

    upward = [(run, run + 1) for run in range(0, run_count - 1, 2)]
    downward = [(run + 1, run) for run in range(0, run_count - 1, 2)]
    two_back = from_behind(kv_local, "qblk", 2)
    low = lax.ppermute(kv_local, "qblk", upward)
    own_vertical, bias = lax.optimization_barrier((own_vertical, bias))
    vertical = sum_up_to_here(own_vertical)
    two_back, vertical = lax.optimization_barrier((two_back, vertical))
    high = lax.ppermute(two_back, "qblk", downward)
    q_local = lax.all_to_all(queries, "head", split_axis=1, concat_axis=0, tiled=True)
    parts = []
    for kv in range(kv_heads):
        heads = slice(kv * group, (kv + 1) * group)
        attended = attend(
            q_local,
            two_back,
            low,
            high,
            kv_local,
            odd,
            vertical,
            slash_mine[heads],
            bias,
            kv,
            kv_heads,
        )
        parts.append(lax.all_to_all(attended, "head", split_axis=0, concat_axis=0, tiled=True))
    return lay_columns(parts, head_count)


def solution(mesh):
    return jax.shard_map(
        per_device,
        mesh=mesh,
        in_specs=(
            P(("qblk", "head"), None),
            P(("qblk", "head"), None),
            P(("qblk", "head"), None),
            P(),
            P(),
        ),
        out_specs=P(("qblk", "head"), None),
        check_vma=False,
    )
```
